256 devices in a mesh: year: 8 (over x, core), word: 8 (over z), context: 4 (over y).
Axes of the slice: x: 4, y: 4, z: 8, core: 2. Of those that a mesh axis runs over, the one named last changes fastest.
Arguments:
- slices: bfloat16 [16, 8192, 8192], P('year', 'word', 'context'), may hold values from -60 to 60
- context_factor: bfloat16 [8192, 256], P('context'), may hold values from -0.0625 to 0.0625
- mixing: float32 [256, 256], replicated, may hold values from -0.12 to 2.5
- year_weights: float32 [16, 256], replicated, may hold values from 0.5 to 2
Outputs:
- new_mixing: float32 [256, 256], replicated
- new_context: float32 [8192, 256], P('context')
- new_years: float32 [16, 256], replicated
The draws below stay inside these ranges and needn't reach their ends.
All inputs are finite; a program needn't handle non-finite values.
Results may differ from the reference program's by a relative error of at most 0.0027.
Values may be sent and summed in bfloat16 or wider, within the bound.
No kernel may reach another device: no remote copies, remote signals or barrier semaphores. Data moves between devices by JAX's collectives and lax.ppermute only.
A program may use at most 128 MiB of HBM per device.

```python
import math
import jax
import jax.numpy as jnp
from jax import lax

WORDS = 8192
CONTEXTS = 8192
RANK = 256
NS_STEPS = 8
YEARS = 16


def draw_slices(key, part):
    key = jax.random.fold_in(key, 11)
    noise_key, row_key, column_key, year_key = jax.random.split(key, 4)
    spread = 0.5 * math.log(10.0)
    row_scale = jnp.exp(jax.random.uniform(row_key, (YEARS, WORDS, 1), jnp.float32, -spread, spread))
    column_scale = jnp.exp(jax.random.uniform(column_key, (YEARS, 1, CONTEXTS), jnp.float32, -spread, spread))
    year_scale = jnp.exp(jax.random.uniform(year_key, (YEARS, 1, 1), jnp.float32, -0.35, 0.35))
    noise_values = jnp.clip(jax.random.normal(noise_key, (YEARS, WORDS, CONTEXTS), jnp.float32), -4.0, 4.0)
    return (noise_values * row_scale * column_scale * year_scale).astype(jnp.bfloat16)


def draw_mixing(key, part):
    key = jax.random.fold_in(key, 23)
    diagonal_key, offdiag_key = jax.random.split(key, 2)
    diagonal = jax.random.uniform(diagonal_key, (RANK,), jnp.float32, 1.5, 2.5)
    offdiag = 0.03 * jnp.clip(jax.random.normal(offdiag_key, (RANK, RANK), jnp.float32), -4.0, 4.0)
    positions = jnp.arange(RANK)
    eye_mask = (positions[:, None] == positions[None, :]).astype(jnp.float32)
    return offdiag * (1.0 - eye_mask) + eye_mask * diagonal[None, :]


def block_levels(own_key, shape, pieces, smallest, top_value):
    loudness = 1.0
    for dim, parts in pieces:
        steps = jax.random.uniform(jax.random.fold_in(jax.random.fold_in(own_key, 6), dim), (parts,), jnp.float32, smallest / len(pieces), top_value / len(pieces))
        loudness = loudness * jnp.repeat(jnp.exp(steps), shape[dim] // parts).reshape((-1,) + (1,) * (len(shape) - 1 - dim))
    return loudness


def noise(stream_key, extent, width, limit, cuts=(), dtype=jnp.bfloat16):
    result = jax.random.normal(stream_key, extent, jnp.float32) * width
    if len(cuts) > 0:
        result = block_levels(stream_key, extent, cuts, -0.22, 0.18) * result
    return jnp.clip(result, min=-limit, max=limit).astype(dtype)


def setup_inputs(seed: int = 0) -> dict:
    keys = jax.random.split(jax.random.key(seed), 5)
    return {
        "slices": draw_slices(jax.random.fold_in(keys[4], 71), 0),
        "context_factor": noise(keys[1], (CONTEXTS, RANK), CONTEXTS ** -0.5, 0.0625, ((0, 4),)),
        "mixing": draw_mixing(jax.random.fold_in(keys[4], 71), 0),
        "year_weights": jnp.clip(jnp.exp(jax.random.uniform(keys[3], (YEARS, RANK), jnp.float32, math.log(0.5), math.log(2.0))), 0.5, 2.0),
    }


HIGHEST = lax.Precision.HIGHEST

def solve_rows(gram_matrix, right_side):
    lower_factor = jnp.linalg.cholesky(gram_matrix)
    return jax.scipy.linalg.cho_solve((lower_factor, True), right_side.T).T

def polar_factor(target):
    squares = jnp.sum(target * target)
    iterate = target / jnp.sqrt(squares + 1e-06)
    for sweep_index in range(NS_STEPS):
        gram_now = jnp.dot(iterate.T.astype(jnp.float32), iterate.astype(jnp.float32), precision=HIGHEST, preferred_element_type=jnp.float32)
        iterate = 1.5 * iterate - 0.5 * jnp.dot(iterate.astype(jnp.float32), gram_now.astype(jnp.float32), precision=HIGHEST, preferred_element_type=jnp.float32)
    return iterate

def reference(slices, context_factor, mixing, year_weights):

    def one_year(carry, inputs):
        mixing_sum, context_sum = carry
        year_slice, weights_now = inputs
        coupled = (weights_now[:, None] * mixing.T).astype(jnp.bfloat16)
        reduced = jnp.dot(year_slice.astype(jnp.float32), context_factor.astype(jnp.float32), preferred_element_type=jnp.float32)
        target = jnp.dot(reduced.astype(jnp.float32), coupled.astype(jnp.float32), precision=HIGHEST, preferred_element_type=jnp.float32)
        frames = polar_factor(target).astype(jnp.bfloat16)
        through = jnp.dot(frames.astype(jnp.float32).T.astype(jnp.float32), reduced.astype(jnp.float32), precision=HIGHEST, preferred_element_type=jnp.float32)
        weighted = (mixing * weights_now[None, :]).astype(jnp.bfloat16)
        lifted = jnp.dot(frames.astype(jnp.float32), weighted.astype(jnp.float32), preferred_element_type=jnp.float32).astype(jnp.bfloat16)
        mixing_sum = mixing_sum + weights_now[None, :] * through
        context_sum = context_sum + jnp.dot(year_slice.T.astype(jnp.float32), lifted.astype(jnp.float32), preferred_element_type=jnp.float32)
        year_term = lax.optimization_barrier(jnp.sum(mixing * through, axis=0))
        return ((mixing_sum, context_sum), year_term)
    start_carry = (jnp.zeros((RANK, RANK), jnp.float32), jnp.zeros((CONTEXTS, RANK), jnp.float32))
    (mixing_term, context_term), years_term = lax.scan(one_year, start_carry, (slices, year_weights))
    factor_gram = jnp.dot(context_factor.T.astype(jnp.float32), context_factor.astype(jnp.float32), preferred_element_type=jnp.float32)
    weight_gram = jnp.dot(year_weights.T.astype(jnp.float32), year_weights.astype(jnp.float32), precision=HIGHEST, preferred_element_type=jnp.float32)
    mixing_gram = jnp.dot(mixing.T.astype(jnp.float32), mixing.astype(jnp.float32), precision=HIGHEST, preferred_element_type=jnp.float32)
    new_mixing = solve_rows(factor_gram * weight_gram, mixing_term)
    new_context = solve_rows(mixing_gram * weight_gram, context_term)
    new_years = solve_rows(mixing_gram * factor_gram, years_term)
    return (new_mixing, new_context, new_years)
```

```python
import functools

import jax
import jax.numpy as jnp
from jax import lax
from jax.experimental import pallas as pl
from jax.experimental.pallas import tpu as pltpu
from jax.sharding import Mesh, PartitionSpec as P

NS_STEPS = 8
F32, BF16 = jnp.float32, jnp.bfloat16
HIGHEST = lax.Precision.HIGHEST
VMEM_BYTES = 48 * 1024 * 1024
VMEM_SPEC = pl.BlockSpec(memory_space=pltpu.VMEM)
SMEM_SPEC = pl.BlockSpec(memory_space=pltpu.SMEM)
ANY_SPEC = pl.BlockSpec(memory_space=pl.ANY)


def dot(a, b, contract=((1,), (0,)), precision=None):
    return lax.dot_general(a, b, (contract, ((), ())), precision=precision, preferred_element_type=F32)


def exact(a, b, contract=((1,), (0,))):
    return dot(a, b, contract, HIGHEST)


def halves(a):
    high = a.astype(BF16)
    return high, (a - high.astype(F32)).astype(BF16)


def close(a, b):
    return dot(a[0], b[0]) + (dot(a[0], b[1]) + dot(a[1], b[0]))


def params():
    return pltpu.CompilerParams(vmem_limit_bytes=VMEM_BYTES)


def reduced_kernel(parts, me_ref, slices_ref, factor_ref, *out_refs):
    step = pl.program_id(0)
    products = [dot(slices_ref[y], factor_ref[...]) for y in range(slices_ref.shape[0])]
    for shift in range(parts):

        @pl.when(step == shift)
        def _():
            for y, product in enumerate(products):
                out_refs[shift][y] = product.astype(out_refs[shift].dtype)


def reduced_parts(slices, context_factor, me, parts):
    years, rows, columns = slices.shape
    rank = context_factor.shape[1]
    chunk = rows // parts
    out_block = pl.BlockSpec((years, chunk, rank), lambda s, m: (0, 0, 0))
    return pl.pallas_call(
        functools.partial(reduced_kernel, parts),
        grid_spec=pltpu.PrefetchScalarGridSpec(
            num_scalar_prefetch=1,
            grid=(parts,),
            in_specs=[
                pl.BlockSpec((years, chunk, columns), lambda s, m: (0, lax.rem(m[0] + s, parts), 0)),
                pl.BlockSpec((columns, rank), lambda s, m: (0, 0)),
            ],
            out_specs=[out_block] * parts,
        ),
        out_shape=[
            jax.ShapeDtypeStruct((years, chunk, rank), F32 if s == 0 else BF16) for s in range(parts)
        ],
        compiler_params=params(),
        name="reduced_parts",
    )(me, slices, context_factor)


def factor_share_kernel(at_ref, factor_ref, out_ref, scratch):
    share = out_ref.shape[0]
    scratch[...] = dot(factor_ref[...], factor_ref[...], ((0,), (0,)))
    out_ref[...] = scratch[pl.ds(pl.multiple_of(at_ref[0] * share, share), share), :]


def factor_share(x_me, context_factor, x_count):
    rank = context_factor.shape[1]
    return pl.pallas_call(
        factor_share_kernel,
        in_specs=[SMEM_SPEC, VMEM_SPEC],
        out_specs=VMEM_SPEC,
        out_shape=jax.ShapeDtypeStruct((rank // x_count, rank), F32),
        scratch_shapes=[pltpu.VMEM((rank, rank), F32)],
        compiler_params=params(),
        name="factor_share",
    )(x_me, context_factor)


def sum_parts_kernel(parts, *refs):
    rows, factors = refs[:parts], refs[parts : 2 * parts]
    rows_ref, factor_ref = refs[2 * parts :]
    total = rows[0][...]
    for row in rows[1:]:
        total += row[...].astype(F32)
    rows_ref[...] = total.astype(rows_ref.dtype)
    total = factors[0][...]
    for factor in factors[1:]:
        total += factor[...]
    factor_ref[...] = total


def sum_parts(rows, factors):
    parts = len(rows)
    return pl.pallas_call(
        functools.partial(sum_parts_kernel, parts),
        in_specs=[VMEM_SPEC] * (2 * parts),
        out_specs=[VMEM_SPEC] * 2,
        out_shape=[
            jax.ShapeDtypeStruct(rows[0].shape, BF16),
            jax.ShapeDtypeStruct(factors[0].shape, F32),
        ],
        compiler_params=params(),
        name="sum_parts",
    )(*rows, *factors)


def gram_kernel(parts, factor_parts, at_ref, *refs):
    pieces, factors = refs[:parts], refs[parts : parts + factor_parts]
    out_ref, factor_ref, scratch = refs[parts + factor_parts :]
    words, years, share, rank = out_ref.shape
    first = at_ref[0] * (words * share)
    for y in range(years):
        total = dot(pieces[0][y], pieces[0][y], ((0,), (0,)))
        for piece in pieces[1:]:
            total += dot(piece[y], piece[y], ((0,), (0,)))
        scratch[...] = total
        for w in range(words):
            out_ref[w, y] = scratch[pl.ds(pl.multiple_of(first + w * share, share), share), :]
    height = factors[0].shape[0]
    for shift, factor in enumerate(factors):
        owner = lax.rem(at_ref[1] + (factor_parts - shift), factor_parts)
        factor_ref[pl.ds(pl.multiple_of(owner * height, height), height), :] = factor[...]


def gram_share(pieces, factors, at, words):
    parts, factor_parts = len(pieces), len(factors)
    years, _, rank = pieces[0].shape
    share = rank // (parts * words)
    return pl.pallas_call(
        functools.partial(gram_kernel, parts, factor_parts),
        in_specs=[SMEM_SPEC] + [VMEM_SPEC] * (parts + factor_parts),
        out_specs=[VMEM_SPEC] * 2,
        out_shape=[
            jax.ShapeDtypeStruct((words, years, share, rank), F32),
            jax.ShapeDtypeStruct((rank, rank), F32),
        ],
        scratch_shapes=[pltpu.VMEM((rank, rank), F32)],
        compiler_params=params(),
        name="gram_share",
    )(at, *pieces, *factors)


def spread_kernel(after_ref, parts_ref, out_ref):
    total = parts_ref[0]
    for w in range(1, parts_ref.shape[0]):
        total += parts_ref[w]
    for w in range(out_ref.shape[0]):
        out_ref[w] = total


def spread_sum(after, parts):
    return pl.pallas_call(
        spread_kernel,
        in_specs=[ANY_SPEC, VMEM_SPEC],
        out_specs=VMEM_SPEC,
        out_shape=jax.ShapeDtypeStruct(parts.shape, parts.dtype),
        compiler_params=params(),
        name="spread_sum",
    )(after, parts)


PANEL = 8


def sweep_panel(panel, first):
    lanes = lax.broadcasted_iota(jnp.int32, panel.shape, 1)
    rows = lax.broadcasted_iota(jnp.int32, panel.shape, 0)
    for j in range(PANEL):
        column = panel[:, first + j : first + j + 1]
        inverse = 1.0 / panel[j : j + 1, first + j : first + j + 1]
        scaled = panel[j : j + 1, :] * inverse
        at_pivot = lanes == first + j
        others = jnp.where(at_pivot, -column * inverse, panel - column * scaled)
        panel = jnp.where(rows == j, jnp.where(at_pivot, inverse, scaled), others)
    return panel


def minus_inverses(blocks):
    size = blocks[0].shape[0]
    lanes = lax.broadcasted_iota(jnp.int32, (PANEL, size), 1)
    rows = lax.broadcasted_iota(jnp.int32, (PANEL, size), 0)
    all_lanes = lax.broadcasted_iota(jnp.int32, (size, size), 1)
    all_rows = lax.broadcasted_iota(jnp.int32, (size, size), 0)
    for first in range(0, size, PANEL):
        inside = (lanes >= first) & (lanes < first + PANEL)
        outside = ((all_lanes < first) | (all_lanes >= first + PANEL)) & (
            (all_rows < first) | (all_rows >= first + PANEL)
        )
        unit = jnp.where(lanes == rows + first, 1.0, 0.0)
        panels = [block[first : first + PANEL, :] for block in blocks]
        swept = [sweep_panel(panel, first) for panel in panels]
        for b in range(len(blocks)):
            rest = jnp.where(inside, 0.0, swept[b])
            left = jnp.concatenate([jnp.where(inside, 0.0, -panels[b]), unit, rest], axis=0)
            right = jnp.concatenate([rest, jnp.where(inside, -swept[b], swept[b]), unit], axis=0)
            blocks[b] = jnp.where(outside, blocks[b], 0.0) + exact(left, right, ((0,), (0,)))
    return blocks


def inverse_first_kernel(factor_ref, mixing_ref, weights_ref, first_ref, cross_ref, rest_ref):
    mixing_gram = exact(mixing_ref[...], mixing_ref[...], ((0,), (0,)))
    weight_gram = exact(weights_ref[...], weights_ref[...], ((0,), (0,)))
    factor_gram = factor_ref[...]
    grams = [mixing_gram * weight_gram, factor_gram * weight_gram, mixing_gram * factor_gram]
    half = factor_gram.shape[0] // 2
    swept = minus_inverses([gram[:half, :half] for gram in grams])
    for b, gram in enumerate(grams):
        cross = exact(-swept[b], gram[:half, half:])
        first_ref[b] = -swept[b]
        cross_ref[b] = cross
        rest_ref[b] = gram[half:, half:] - exact(gram[:half, half:], cross, ((0,), (0,)))


def inverse_first(factor_gram, mixing, year_weights):
    half = mixing.shape[0] // 2
    return pl.pallas_call(
        inverse_first_kernel,
        in_specs=[VMEM_SPEC] * 3,
        out_specs=[VMEM_SPEC] * 3,
        out_shape=[jax.ShapeDtypeStruct((3, half, half), F32)] * 3,
        compiler_params=params(),
        name="inverse_first",
    )(factor_gram, mixing, year_weights)


def inverse_last_kernel(after_ref, first_ref, cross_ref, rest_ref, weighted_ref, lift_ref, *inverse_refs):
    half = first_ref.shape[1]
    swept = minus_inverses([rest_ref[b] for b in range(3)])
    for b in range(3):
        target = inverse_refs[b]
        last = -swept[b]
        upper = -exact(cross_ref[b], last)
        target[:half, :half] = first_ref[b] - exact(upper, cross_ref[b], ((1,), (1,)))
        target[:half, half:] = upper
        target[half:, :half] = upper.T
        target[half:, half:] = last
    for y in range(weighted_ref.shape[0]):
        lift_ref[y] = exact(weighted_ref[y].astype(F32), inverse_refs[0][...])


def inverse_last(after, first, cross, rest, weighted):
    rank = weighted.shape[-1]
    inverse = jax.ShapeDtypeStruct((rank, rank), F32)
    return pl.pallas_call(
        inverse_last_kernel,
        in_specs=[ANY_SPEC] + [VMEM_SPEC] * 4,
        out_specs=[VMEM_SPEC] * 4,
        out_shape=[jax.ShapeDtypeStruct(weighted.shape, F32)] + [inverse] * 3,
        compiler_params=params(),
        name="inverse_last",
    )(after, first, cross, rest, weighted)


def frames_kernel(parts, at_ref, slices_ref, *refs):
    grams, rows = refs[:parts], refs[parts : 2 * parts]
    coupled_ref, lift_ref, weights_ref, mixing_ref = refs[2 * parts : 2 * parts + 4]
    keep_ref, give_ref, side_ref = refs[2 * parts + 4 : 2 * parts + 7]
    tile_ref, gram_ref, rows_ref, lifted_ref, sem = refs[2 * parts + 7 :]
    years, tile_rows, columns = tile_ref.shape
    rank = mixing_ref.shape[0]
    load = pltpu.make_async_copy(slices_ref, tile_ref, sem)
    load.start()
    me, core, year_first = at_ref[0], at_ref[1], at_ref[2]
    words, _, share, _ = grams[0].shape
    chunk = rows[0].shape[1]
    for shift in range(parts):
        owner = lax.rem(me + (parts - shift), parts)
        for y in range(years):
            for w in range(words):
                at = pl.multiple_of(owner * (words * share) + w * share, share)
                gram_ref[y, pl.ds(at, share), :] = grams[shift][w, y]
            at = pl.multiple_of(owner * chunk, chunk)
            rows_ref[y, pl.ds(at, chunk), :] = rows[shift][y]

    row_at = lax.broadcasted_iota(jnp.int32, (rank, rank), 0)
    diagonal = row_at == lax.broadcasted_iota(jnp.int32, (rank, rank), 1)
    coupled = [coupled_ref[y].astype(F32) for y in range(years)]
    half_way = [exact(coupled[y], gram_ref[y], ((0,), (0,))) for y in range(years)]
    squares = [exact(half_way[y], coupled[y]) for y in range(years)]
    traces = [
        jnp.sum(jnp.sum(jnp.where(diagonal, s, 0.0), axis=1, keepdims=True), axis=0, keepdims=True) + 1e-06
        for s in squares
    ]
    gram_now = [squares[y] / traces[y] for y in range(years)]
    polar = [None] * years
    for sweep in range(NS_STEPS):
        factor = [jnp.where(diagonal, 1.5, 0.0) - 0.5 * g for g in gram_now]
        split = [halves(f) for f in factor]
        polar = [factor[y] if sweep == 0 else close(halves(polar[y]), split[y]) for y in range(years)]
        if sweep < NS_STEPS - 1:
            gram_now = [close(halves(gram_now[y]), split[y]) for y in range(years)]
            gram_now = [close(halves(gram_now[y]), split[y]) for y in range(years)]
    scale = [lax.rsqrt(t) for t in traces]
    lift = [exact(coupled[y], exact(polar[y], lift_ref[y])) * scale[y] for y in range(years)]
    side_ref[rank:, :] = jnp.zeros((side_ref.shape[0] - rank, rank), F32)
    mixing_part = None
    for y in range(years):
        through = exact(polar[y], half_way[y], ((0,), (0,))) * scale[y]
        term = weights_ref[pl.ds(year_first + y, 1), :] * through
        mixing_part = term if mixing_part is None else mixing_part + term
        side_ref[pl.ds(rank + year_first + y, 1), :] = jnp.sum(
            mixing_ref[...] * through, axis=0, keepdims=True
        )
    side_ref[:rank, :] = mixing_part
    for y in range(years):
        high, low = halves(lift[y])
        lifted = dot(high, rows_ref[y], ((0,), (1,))) + dot(low, rows_ref[y], ((0,), (1,)))
        lifted_ref[:, y * tile_rows : (y + 1) * tile_rows] = lifted.astype(BF16)
    load.wait()
    half = columns // 2
    width = rank
    for target, side in ((give_ref, 1 - core), (keep_ref, core)):
        for first in range(0, half, width):
            at = pl.multiple_of(side * half + first, width)
            total = dot(lifted_ref[:, :tile_rows], tile_ref[0, :, pl.ds(at, width)])
            for y in range(1, years):
                total += dot(
                    lifted_ref[:, y * tile_rows : (y + 1) * tile_rows], tile_ref[y, :, pl.ds(at, width)]
                )
            target[first : first + width, :] = total.T.astype(target.dtype)


def frames_and_context(at, slices, grams, rows, coupled, lift, year_weights, mixing):
    parts = len(grams)
    years, tile_rows, columns = slices.shape
    rank = mixing.shape[0]
    side_rows = rank + year_weights.shape[0]
    return pl.pallas_call(
        functools.partial(frames_kernel, parts),
        in_specs=[SMEM_SPEC, ANY_SPEC] + [VMEM_SPEC] * (2 * parts + 4),
        out_specs=[VMEM_SPEC] * 3,
        out_shape=[
            jax.ShapeDtypeStruct((columns // 2, rank), F32),
            jax.ShapeDtypeStruct((columns // 2, rank), BF16),
            jax.ShapeDtypeStruct((side_rows, rank), F32),
        ],
        scratch_shapes=[
            pltpu.VMEM((years, tile_rows, columns), BF16),
            pltpu.VMEM((years, rank, rank), F32),
            pltpu.VMEM((years, tile_rows, rank), BF16),
            pltpu.VMEM((rank, years * tile_rows), BF16),
            pltpu.SemaphoreType.DMA(()),
        ],
        compiler_params=params(),
        name="frames_and_context",
    )(at, slices, *grams, *rows, coupled, lift, year_weights, mixing)


def finish_kernel(parts, *refs):
    context_ref, sides = refs[0], refs[1 : 1 + parts]
    first_ref, second_ref, spread_ref, mixing_ref, years_ref = refs[1 + parts :]
    count = context_ref.shape[0]
    total = context_ref[0].astype(F32)
    for i in range(1, count):
        total += context_ref[i].astype(F32)
    for i in range(count):
        spread_ref[i] = total
    side = sides[0][...]
    for piece in sides[1:]:
        side += piece[...]
    rank = first_ref.shape[0]
    mixing_ref[...] = exact(side[:rank], first_ref[...])
    years_ref[...] = exact(side[rank:], second_ref[...])


def finish(context_parts, sides, first_inverse, second_inverse):
    parts = len(sides)
    side_rows, rank = sides[0].shape
    return pl.pallas_call(
        functools.partial(finish_kernel, parts),
        in_specs=[VMEM_SPEC] * (3 + parts),
        out_specs=[VMEM_SPEC] * 3,
        out_shape=[
            jax.ShapeDtypeStruct(context_parts.shape, F32),
            jax.ShapeDtypeStruct((rank, rank), F32),
            jax.ShapeDtypeStruct((side_rows - rank, rank), F32),
        ],
        compiler_params=params(),
        name="finish",
    )(context_parts, *sides, first_inverse, second_inverse)


def around(value, axis):
    size = lax.axis_size(axis)
    return [value] + [
        lax.ppermute(value, axis, [(i, (i + shift) % size) for i in range(size)]) for shift in range(1, size)
    ]


def local(slices, context_factor, mixing, year_weights):
    years_here = slices.shape[0]
    rank = mixing.shape[0]
    x_count, cores = lax.axis_size("x"), lax.axis_size("core")
    word_count, parts = lax.axis_size("word"), lax.axis_size("context")
    x_me, core, me = lax.axis_index("x"), lax.axis_index("core"), lax.axis_index("context")
    year_first = (x_me * cores + core) * years_here
    at = jnp.stack([me, core, year_first]).astype(jnp.int32)
    local_weights = lax.dynamic_slice_in_dim(year_weights, year_first, years_here, 0)
    coupled = (local_weights[:, :, None] * mixing.T[None, :, :]).astype(BF16)
    weighted = (mixing[None, :, :] * local_weights[:, None, :]).astype(BF16)

    sent = reduced_parts(slices, context_factor, at[:1], parts)
    arrived = [
        lax.ppermute(sent[shift], "context", [(i, (i + shift) % parts) for i in range(parts)])
        for shift in range(1, parts)
    ]
    factor_arrived = around(factor_share(x_me.astype(jnp.int32)[None], context_factor, x_count), "context")
    own_rows, factor_rows = sum_parts([sent[0]] + arrived, factor_arrived)
    rows = around(own_rows, "context")
    factor_pieces = around(factor_rows, "x")

    gram_part, factor_gram = gram_share(
        rows, factor_pieces, jnp.stack([me, x_me]).astype(jnp.int32), word_count
    )
    gram_part = lax.all_to_all(gram_part, "word", 0, 0, tiled=True)
    first, cross, rest = inverse_first(factor_gram, mixing, year_weights)
    spread = spread_sum(rest, gram_part)
    lift, _, first_inverse, second_inverse = inverse_last(spread, first, cross, rest, weighted)
    grams = around(lax.all_to_all(spread, "word", 0, 0, tiled=True), "context")

    keep, give, side = frames_and_context(
        at, slices, grams, rows, coupled, lift, year_weights, mixing
    )

    swap = [(i, cores - 1 - i) for i in range(cores)]
    both = keep + lax.ppermute(give, "core", swap).astype(F32)
    count = x_count * word_count
    both = both.astype(BF16).reshape(count, -1, rank)
    both = lax.all_to_all(both, ("x", "word"), 0, 0, tiled=True)
    sides = around(side + lax.ppermute(side, "core", swap), "x")
    summed, new_mixing, new_years = finish(both, sides, first_inverse, second_inverse)
    mine = lax.all_to_all(summed, ("x", "word"), 0, 0, tiled=True).reshape(-1, rank)
    other = lax.ppermute(mine, "core", swap)
    new_context = jnp.where(
        core == 0, jnp.concatenate([mine, other]), jnp.concatenate([other, mine])
    )
    return (new_mixing, new_context, new_years)


def solution(mesh):
    year_count, word_count, context_count = mesh.devices.shape
    cores = 2
    fine = Mesh(
        mesh.devices.reshape(year_count // cores, cores, word_count, context_count),
        ("x", "core", "word", "context"),
    )
    in_specs = (P(("x", "core"), "word", "context"), P("context", None), P(), P())
    out_specs = (P(), P("context", None), P())
    return jax.shard_map(local, mesh=fine, in_specs=in_specs, out_specs=out_specs, check_vma=False)
```

```python
import functools

import jax
import jax.numpy as jnp
from jax import lax
from jax.experimental import pallas as pl
from jax.experimental.pallas import tpu as pltpu
from jax.sharding import Mesh, PartitionSpec as P

NS_STEPS = 8
F32, BF16 = jnp.float32, jnp.bfloat16
HIGHEST = lax.Precision.HIGHEST
VMEM_BYTES = 48 * 1024 * 1024
VMEM_SPEC = pl.BlockSpec(memory_space=pltpu.VMEM)
SMEM_SPEC = pl.BlockSpec(memory_space=pltpu.SMEM)
ANY_SPEC = pl.BlockSpec(memory_space=pl.ANY)


def dot(a, b, contract=((1,), (0,)), precision=None):
    return lax.dot_general(a, b, (contract, ((), ())), precision=precision, preferred_element_type=F32)


def exact(a, b, contract=((1,), (0,))):
    return dot(a, b, contract, HIGHEST)


def halves(a):
    high = a.astype(BF16)
    return high, (a - high.astype(F32)).astype(BF16)


def close(a, b):
    return dot(a[0], b[0]) + (dot(a[0], b[1]) + dot(a[1], b[0]))


def params():
    return pltpu.CompilerParams(vmem_limit_bytes=VMEM_BYTES)


def reduced_kernel(parts, me_ref, slices_ref, factor_ref, *out_refs):
    step = pl.program_id(0)
    products = [dot(slices_ref[y], factor_ref[...]) for y in range(slices_ref.shape[0])]
    for shift in range(parts):

        @pl.when(step == shift)
        def _():
            for y, product in enumerate(products):
                out_refs[shift][y] = product.astype(out_refs[shift].dtype)


def reduced_parts(slices, context_factor, me, parts):
    years, rows, columns = slices.shape
    rank = context_factor.shape[1]
    chunk = rows // parts
    out_block = pl.BlockSpec((years, chunk, rank), lambda s, m: (0, 0, 0))
    return pl.pallas_call(
        functools.partial(reduced_kernel, parts),
        grid_spec=pltpu.PrefetchScalarGridSpec(
            num_scalar_prefetch=1,
            grid=(parts,),
            in_specs=[
                pl.BlockSpec((years, chunk, columns), lambda s, m: (0, lax.rem(m[0] + s, parts), 0)),
                pl.BlockSpec((columns, rank), lambda s, m: (0, 0)),
            ],
            out_specs=[out_block] * parts,
        ),
        out_shape=[
            jax.ShapeDtypeStruct((years, chunk, rank), F32 if s == 0 else BF16) for s in range(parts)
        ],
        compiler_params=params(),
        name="reduced_parts",
    )(me, slices, context_factor)


def factor_share_kernel(at_ref, factor_ref, out_ref, scratch):
    share = out_ref.shape[0]
    scratch[...] = dot(factor_ref[...], factor_ref[...], ((0,), (0,)))
    out_ref[...] = scratch[pl.ds(pl.multiple_of(at_ref[0] * share, share), share), :]


def factor_share(x_me, context_factor, x_count):
    rank = context_factor.shape[1]
    return pl.pallas_call(
        factor_share_kernel,
        in_specs=[SMEM_SPEC, VMEM_SPEC],
        out_specs=VMEM_SPEC,
        out_shape=jax.ShapeDtypeStruct((rank // x_count, rank), F32),
        scratch_shapes=[pltpu.VMEM((rank, rank), F32)],
        compiler_params=params(),
        name="factor_share",
    )(x_me, context_factor)


def sum_parts_kernel(parts, after_ref, *refs):
    rows, factors = refs[:parts], refs[parts : 2 * parts]
    rows_ref, factor_ref = refs[2 * parts :]
    total = rows[0][...]
    for row in rows[1:]:
        total += row[...].astype(F32)
    rows_ref[...] = total.astype(rows_ref.dtype)
    total = factors[0][...]
    for factor in factors[1:]:
        total += factor[...]
    factor_ref[...] = total


def sum_parts(after, rows, factors):
    parts = len(rows)
    return pl.pallas_call(
        functools.partial(sum_parts_kernel, parts),
        in_specs=[ANY_SPEC] + [VMEM_SPEC] * (2 * parts),
        out_specs=[VMEM_SPEC] * 2,
        out_shape=[
            jax.ShapeDtypeStruct(rows[0].shape, BF16),
            jax.ShapeDtypeStruct(factors[0].shape, F32),
        ],
        compiler_params=params(),
        name="sum_parts",
    )(after, *rows, *factors)


def gram_kernel(parts, factor_parts, at_ref, *refs):
    pieces, factors = refs[:parts], refs[parts : parts + factor_parts]
    out_ref, factor_ref, scratch = refs[parts + factor_parts :]
    words, years, share, rank = out_ref.shape
    first = at_ref[0] * (words * share)
    for y in range(years):
        total = dot(pieces[0][y], pieces[0][y], ((0,), (0,)))
        for piece in pieces[1:]:
            total += dot(piece[y], piece[y], ((0,), (0,)))
        scratch[...] = total
        for w in range(words):
            out_ref[w, y] = scratch[pl.ds(pl.multiple_of(first + w * share, share), share), :]
    height = factors[0].shape[0]
    for shift, factor in enumerate(factors):
        owner = lax.rem(at_ref[1] + (factor_parts - shift), factor_parts)
        factor_ref[pl.ds(pl.multiple_of(owner * height, height), height), :] = factor[...]


def gram_share(pieces, factors, at, words):
    parts, factor_parts = len(pieces), len(factors)
    years, _, rank = pieces[0].shape
    share = rank // (parts * words)
    return pl.pallas_call(
        functools.partial(gram_kernel, parts, factor_parts),
        in_specs=[SMEM_SPEC] + [VMEM_SPEC] * (parts + factor_parts),
        out_specs=[VMEM_SPEC] * 2,
        out_shape=[
            jax.ShapeDtypeStruct((words, years, share, rank), F32),
            jax.ShapeDtypeStruct((rank, rank), F32),
        ],
        scratch_shapes=[pltpu.VMEM((rank, rank), F32)],
        compiler_params=params(),
        name="gram_share",
    )(at, *pieces, *factors)


def spread_kernel(parts_ref, out_ref):
    total = parts_ref[0]
    for w in range(1, parts_ref.shape[0]):
        total += parts_ref[w]
    for w in range(out_ref.shape[0]):
        out_ref[w] = total


def spread_sum(parts):
    return pl.pallas_call(
        spread_kernel,
        in_specs=[VMEM_SPEC],
        out_specs=VMEM_SPEC,
        out_shape=jax.ShapeDtypeStruct(parts.shape, parts.dtype),
        compiler_params=params(),
        name="spread_sum",
    )(parts)


NEWTON_MOST = 48
NEWTON_SETTLED = 4e-8


def identity(size):
    rows = lax.broadcasted_iota(jnp.int32, (size, size), 0)
    return jnp.where(rows == lax.broadcasted_iota(jnp.int32, (size, size), 1), 1.0, 0.0)


def inverses(grams, scaled_ref, guess_ref, rest_ref):
    count, size = len(grams), grams[0].shape[0]
    eye = identity(size)
    scales = []

    def residual():
        most = None
        for b in range(count):
            rest = eye - exact(scaled_ref[b], guess_ref[b])
            rest_ref[b] = rest
            square = jnp.sum(rest * rest)
            most = square if most is None else jnp.maximum(most, square)
        return most

    def improve():
        for b in range(count):
            guess = guess_ref[b]
            guess_ref[b] = guess + close(halves(guess), halves(rest_ref[b]))

    for b, gram in enumerate(grams):
        diagonal = gram * eye
        across = lax.rsqrt(jnp.sum(diagonal, axis=0, keepdims=True))
        down = lax.rsqrt(jnp.sum(diagonal, axis=1, keepdims=True))
        scaled = gram * across * down
        bound = jnp.max(jnp.sum(jnp.abs(scaled), axis=0, keepdims=True), axis=1, keepdims=True)
        scaled_ref[b] = scaled
        guess_ref[b] = eye / bound
        scales.append((across, down))

    def step(state):
        improve()
        return state[0] + 1, residual()

    lax.while_loop(
        lambda state: (state[0] < NEWTON_MOST) & (state[1] > NEWTON_SETTLED), step, (0, residual())
    )
    improve()
    return [guess_ref[b] * across * down for b, (across, down) in enumerate(scales)]


def newton_scratch(count, rank):
    return [pltpu.VMEM((count, rank, rank), F32)] * 3


def context_inverse_kernel(after_ref, mixing_ref, weights_ref, weighted_ref, lift_ref, *scratch):
    mixing_gram = exact(mixing_ref[...], mixing_ref[...], ((0,), (0,)))
    weight_gram = exact(weights_ref[...], weights_ref[...], ((0,), (0,)))
    (inverse,) = inverses([mixing_gram * weight_gram], *scratch)
    for y in range(weighted_ref.shape[0]):
        lift_ref[y] = exact(weighted_ref[y].astype(F32), inverse)


def context_inverse(after, mixing, year_weights, weighted):
    return pl.pallas_call(
        context_inverse_kernel,
        in_specs=[ANY_SPEC] + [VMEM_SPEC] * 3,
        out_specs=VMEM_SPEC,
        out_shape=jax.ShapeDtypeStruct(weighted.shape, F32),
        scratch_shapes=newton_scratch(1, mixing.shape[0]),
        compiler_params=params(),
        name="context_inverse",
    )(after, mixing, year_weights, weighted)


def factor_inverses_kernel(after_ref, factor_ref, mixing_ref, weights_ref, first_ref, second_ref, *scratch):
    mixing_gram = exact(mixing_ref[...], mixing_ref[...], ((0,), (0,)))
    weight_gram = exact(weights_ref[...], weights_ref[...], ((0,), (0,)))
    factor_gram = factor_ref[...]
    first, second = inverses([factor_gram * weight_gram, mixing_gram * factor_gram], *scratch)
    first_ref[...] = first
    second_ref[...] = second


def factor_inverses(after, factor_gram, mixing, year_weights):
    return pl.pallas_call(
        factor_inverses_kernel,
        in_specs=[ANY_SPEC] + [VMEM_SPEC] * 3,
        out_specs=[VMEM_SPEC] * 2,
        out_shape=[jax.ShapeDtypeStruct(factor_gram.shape, F32)] * 2,
        scratch_shapes=newton_scratch(2, mixing.shape[0]),
        compiler_params=params(),
        name="factor_inverses",
    )(after, factor_gram, mixing, year_weights)


def frames_kernel(parts, at_ref, slices_ref, *refs):
    grams, rows = refs[:parts], refs[parts : 2 * parts]
    coupled_ref, lift_ref, weights_ref, mixing_ref = refs[2 * parts : 2 * parts + 4]
    keep_ref, give_ref, side_ref = refs[2 * parts + 4 : 2 * parts + 7]
    tile_ref, gram_ref, rows_ref, lifted_ref, sem = refs[2 * parts + 7 :]
    years, tile_rows, columns = tile_ref.shape
    rank = mixing_ref.shape[0]
    load = pltpu.make_async_copy(slices_ref, tile_ref, sem)
    load.start()
    me, core, year_first = at_ref[0], at_ref[1], at_ref[2]
    words, _, share, _ = grams[0].shape
    chunk = rows[0].shape[1]
    for shift in range(parts):
        owner = lax.rem(me + (parts - shift), parts)
        for y in range(years):
            for w in range(words):
                at = pl.multiple_of(owner * (words * share) + w * share, share)
                gram_ref[y, pl.ds(at, share), :] = grams[shift][w, y]
            at = pl.multiple_of(owner * chunk, chunk)
            rows_ref[y, pl.ds(at, chunk), :] = rows[shift][y]

    row_at = lax.broadcasted_iota(jnp.int32, (rank, rank), 0)
    diagonal = row_at == lax.broadcasted_iota(jnp.int32, (rank, rank), 1)
    coupled = [coupled_ref[y].astype(F32) for y in range(years)]
    half_way = [exact(coupled[y], gram_ref[y], ((0,), (0,))) for y in range(years)]
    squares = [exact(half_way[y], coupled[y]) for y in range(years)]
    traces = [
        jnp.sum(jnp.sum(jnp.where(diagonal, s, 0.0), axis=1, keepdims=True), axis=0, keepdims=True) + 1e-06
        for s in squares
    ]
    gram_now = [squares[y] / traces[y] for y in range(years)]
    polar = [None] * years
    for sweep in range(NS_STEPS):
        factor = [jnp.where(diagonal, 1.5, 0.0) - 0.5 * g for g in gram_now]
        split = [halves(f) for f in factor]
        polar = [factor[y] if sweep == 0 else close(halves(polar[y]), split[y]) for y in range(years)]
        if sweep < NS_STEPS - 1:
            gram_now = [close(halves(gram_now[y]), split[y]) for y in range(years)]
            gram_now = [close(halves(gram_now[y]), split[y]) for y in range(years)]
    scale = [lax.rsqrt(t) for t in traces]
    lift = [exact(coupled[y], exact(polar[y], lift_ref[y])) * scale[y] for y in range(years)]
    side_ref[rank:, :] = jnp.zeros((side_ref.shape[0] - rank, rank), F32)
    mixing_part = None
    for y in range(years):
        through = exact(polar[y], half_way[y], ((0,), (0,))) * scale[y]
        term = weights_ref[pl.ds(year_first + y, 1), :] * through
        mixing_part = term if mixing_part is None else mixing_part + term
        side_ref[pl.ds(rank + year_first + y, 1), :] = jnp.sum(
            mixing_ref[...] * through, axis=0, keepdims=True
        )
    side_ref[:rank, :] = mixing_part
    for y in range(years):
        high, low = halves(lift[y])
        lifted = dot(high, rows_ref[y], ((0,), (1,))) + dot(low, rows_ref[y], ((0,), (1,)))
        lifted_ref[:, y * tile_rows : (y + 1) * tile_rows] = lifted.astype(BF16)
    load.wait()
    half = columns // 2
    width = rank
    for target, side in ((give_ref, 1 - core), (keep_ref, core)):
        for first in range(0, half, width):
            at = pl.multiple_of(side * half + first, width)
            total = dot(lifted_ref[:, :tile_rows], tile_ref[0, :, pl.ds(at, width)])
            for y in range(1, years):
                total += dot(
                    lifted_ref[:, y * tile_rows : (y + 1) * tile_rows], tile_ref[y, :, pl.ds(at, width)]
                )
            target[first : first + width, :] = total.T.astype(target.dtype)


def frames_and_context(at, slices, grams, rows, coupled, lift, year_weights, mixing):
    parts = len(grams)
    years, tile_rows, columns = slices.shape
    rank = mixing.shape[0]
    side_rows = rank + year_weights.shape[0]
    return pl.pallas_call(
        functools.partial(frames_kernel, parts),
        in_specs=[SMEM_SPEC, ANY_SPEC] + [VMEM_SPEC] * (2 * parts + 4),
        out_specs=[VMEM_SPEC] * 3,
        out_shape=[
            jax.ShapeDtypeStruct((columns // 2, rank), F32),
            jax.ShapeDtypeStruct((columns // 2, rank), BF16),
            jax.ShapeDtypeStruct((side_rows, rank), F32),
        ],
        scratch_shapes=[
            pltpu.VMEM((years, tile_rows, columns), BF16),
            pltpu.VMEM((years, rank, rank), F32),
            pltpu.VMEM((years, tile_rows, rank), BF16),
            pltpu.VMEM((rank, years * tile_rows), BF16),
            pltpu.SemaphoreType.DMA(()),
        ],
        compiler_params=params(),
        name="frames_and_context",
    )(at, slices, *grams, *rows, coupled, lift, year_weights, mixing)


SCALE_ROWS = 8


def finish_kernel(parts, *refs):
    context_ref, sides = refs[0], refs[1 : 1 + parts]
    first_ref, second_ref, packed_ref, mixing_ref, years_ref = refs[1 + parts :]
    count, height, rank = context_ref.shape
    total = context_ref[0].astype(F32)
    for i in range(1, count):
        total += context_ref[i].astype(F32)
    most = jnp.max(jnp.max(jnp.abs(total), axis=1, keepdims=True), axis=0, keepdims=True)
    power = jnp.clip(jnp.ceil(jnp.log2(most)), -120.0, 120.0)
    total = total * jnp.exp2(-power)
    packed_ref[:height, :] = total[:, : rank // 2]
    packed_ref[height : 2 * height, :] = total[:, rank // 2 :]
    packed_ref[2 * height :, :] = jnp.broadcast_to(power, (SCALE_ROWS, rank // 2))
    side = sides[0][...]
    for piece in sides[1:]:
        side += piece[...]
    mixing_ref[...] = exact(side[:rank], first_ref[...])
    years_ref[...] = exact(side[rank:], second_ref[...])


def finish(context_parts, sides, first_inverse, second_inverse):
    parts = len(sides)
    side_rows, rank = sides[0].shape
    height = context_parts.shape[1]
    return pl.pallas_call(
        functools.partial(finish_kernel, parts),
        in_specs=[VMEM_SPEC] * (3 + parts),
        out_specs=[VMEM_SPEC] * 3,
        out_shape=[
            jax.ShapeDtypeStruct((2 * height + SCALE_ROWS, rank // 2), F32),
            jax.ShapeDtypeStruct((rank, rank), F32),
            jax.ShapeDtypeStruct((side_rows - rank, rank), F32),
        ],
        compiler_params=params(),
        name="finish",
    )(context_parts, *sides, first_inverse, second_inverse)


def around(value, axis):
    size = lax.axis_size(axis)
    return [value] + [
        lax.ppermute(value, axis, [(i, (i + shift) % size) for i in range(size)]) for shift in range(1, size)
    ]


def unpacked(packed):
    count, height, width = packed.shape
    height = (height - SCALE_ROWS) // 2
    value = packed.astype(F32)
    scale = jnp.exp2(value[:, 2 * height : 2 * height + 1, :1])
    value = jnp.concatenate([value[:, :height], value[:, height : 2 * height]], axis=-1)
    return (value * scale).reshape(count * height, 2 * width)


def local(slices, context_factor, mixing, year_weights):
    years_here = slices.shape[0]
    rank = mixing.shape[0]
    x_count, cores = lax.axis_size("x"), lax.axis_size("core")
    word_count, parts = lax.axis_size("word"), lax.axis_size("context")
    x_me, core, me = lax.axis_index("x"), lax.axis_index("core"), lax.axis_index("context")
    year_first = (x_me * cores + core) * years_here
    at = jnp.stack([me, core, year_first]).astype(jnp.int32)
    local_weights = lax.dynamic_slice_in_dim(year_weights, year_first, years_here, 0)
    coupled = (local_weights[:, :, None] * mixing.T[None, :, :]).astype(BF16)
    weighted = (mixing[None, :, :] * local_weights[:, None, :]).astype(BF16)

    sent = reduced_parts(slices, context_factor, at[:1], parts)
    arrived = [
        lax.ppermute(sent[shift], "context", [(i, (i + shift) % parts) for i in range(parts)])
        for shift in range(1, parts)
    ]
    factor_arrived = around(factor_share(x_me.astype(jnp.int32)[None], context_factor, x_count), "context")
    lift = context_inverse(sent[0], mixing, year_weights, weighted)
    own_rows, factor_rows = sum_parts(lift, [sent[0]] + arrived, factor_arrived)
    rows = around(own_rows, "context")
    factor_pieces = around(factor_rows, "x")

    gram_part, factor_gram = gram_share(
        rows, factor_pieces, jnp.stack([me, x_me]).astype(jnp.int32), word_count
    )
    gram_part = lax.all_to_all(gram_part, "word", 0, 0, tiled=True)
    spread = spread_sum(gram_part)
    grams = around(lax.all_to_all(spread, "word", 0, 0, tiled=True), "context")

    keep, give, side = frames_and_context(
        at, slices, grams, rows, coupled, lift, year_weights, mixing
    )

    swap = [(i, cores - 1 - i) for i in range(cores)]
    both = keep + lax.ppermute(give, "core", swap).astype(F32)
    count = x_count * word_count
    both = both.astype(BF16).reshape(count, -1, rank)
    first_inverse, second_inverse = factor_inverses(both, factor_gram, mixing, year_weights)
    both = lax.all_to_all(both, ("x", "word"), 0, 0, tiled=True)
    sides = around(side + lax.ppermute(side, "core", swap), "x")
    packed, new_mixing, new_years = finish(both, sides, first_inverse, second_inverse)
    packed = jnp.broadcast_to(packed.astype(jnp.float16)[None], (count,) + packed.shape)
    mine = lax.all_to_all(packed, ("x", "word"), 0, 0, tiled=True)
    other = lax.ppermute(mine, "core", swap)
    mine, other = unpacked(mine), unpacked(other)
    new_context = jnp.concatenate([jnp.where(core == 0, mine, other), jnp.where(core == 0, other, mine)])
    return (new_mixing, new_context, new_years)


def solution(mesh):
    year_count, word_count, context_count = mesh.devices.shape
    cores = 2
    fine = Mesh(
        mesh.devices.reshape(year_count // cores, cores, word_count, context_count),
        ("x", "core", "word", "context"),
    )
    in_specs = (P(("x", "core"), "word", "context"), P("context", None), P(), P())
    out_specs = (P(), P("context", None), P())
    return jax.shard_map(local, mesh=fine, in_specs=in_specs, out_specs=out_specs, check_vma=False)
```

```python
import functools

import jax
import jax.numpy as jnp
from jax import lax
from jax.experimental import pallas as pl
from jax.experimental.pallas import tpu as pltpu
from jax.sharding import Mesh, PartitionSpec as P

NS_STEPS = 8
F32, BF16 = jnp.float32, jnp.bfloat16
HIGHEST = lax.Precision.HIGHEST
VMEM_BYTES = 48 * 1024 * 1024
VMEM_SPEC = pl.BlockSpec(memory_space=pltpu.VMEM)
SMEM_SPEC = pl.BlockSpec(memory_space=pltpu.SMEM)
ANY_SPEC = pl.BlockSpec(memory_space=pl.ANY)


def dot(a, b, contract=((1,), (0,)), precision=None):
    return lax.dot_general(a, b, (contract, ((), ())), precision=precision, preferred_element_type=F32)


def exact(a, b, contract=((1,), (0,))):
    return dot(a, b, contract, HIGHEST)


def halves(a):
    high = a.astype(BF16)
    return high, (a - high.astype(F32)).astype(BF16)


def thirds(a):
    high, rest = halves(a)
    return high, rest, (a - high.astype(F32) - rest.astype(F32)).astype(BF16)


def close(a, b, contract=((1,), (0,))):
    return dot(a[0], b[0], contract) + (dot(a[0], b[1], contract) + dot(a[1], b[0], contract))


def params():
    return pltpu.CompilerParams(vmem_limit_bytes=VMEM_BYTES)


def reduced_kernel(count, me_ref, slices_ref, factor_ref, *out_refs):
    step = pl.program_id(0)
    products = [dot(slices_ref[y], factor_ref[...]) for y in range(slices_ref.shape[0])]
    for i in range(count):

        @pl.when(step == i)
        def _():
            for y, product in enumerate(products):
                out_refs[i][y] = product.astype(out_refs[i].dtype)


def reduced_parts(slices, context_factor, me, parts, shifts, dtype):
    first, stride, count = shifts
    years, rows, columns = slices.shape
    rank = context_factor.shape[1]
    chunk = rows // parts
    out_block = pl.BlockSpec((years, chunk, rank), lambda s, m: (0, 0, 0))
    return pl.pallas_call(
        functools.partial(reduced_kernel, count),
        grid_spec=pltpu.PrefetchScalarGridSpec(
            num_scalar_prefetch=1,
            grid=(count,),
            in_specs=[
                pl.BlockSpec(
                    (years, chunk, columns), lambda s, m: (0, lax.rem(m[0] + first + s * stride, parts), 0)
                ),
                pl.BlockSpec((columns, rank), lambda s, m: (0, 0)),
            ],
            out_specs=[out_block] * count,
        ),
        out_shape=[jax.ShapeDtypeStruct((years, chunk, rank), dtype)] * count,
        compiler_params=params(),
        name="reduced_parts",
    )(me, slices, context_factor)


def factor_share_kernel(at_ref, after_ref, factor_ref, out_ref, scratch):
    share = out_ref.shape[0]
    scratch[...] = dot(factor_ref[...], factor_ref[...], ((0,), (0,)))
    out_ref[...] = scratch[pl.ds(pl.multiple_of(at_ref[0] * share, share), share), :]


def factor_share(me, after, context_factor, shares):
    rank = context_factor.shape[1]
    return pl.pallas_call(
        factor_share_kernel,
        in_specs=[SMEM_SPEC, ANY_SPEC, VMEM_SPEC],
        out_specs=VMEM_SPEC,
        out_shape=jax.ShapeDtypeStruct((rank // shares, rank), F32),
        scratch_shapes=[pltpu.VMEM((rank, rank), F32)],
        compiler_params=params(),
        name="factor_share",
    )(me, after, context_factor)


def rows_kernel(me_ref, *refs):
    count = (len(refs) - 2) // 2
    parts, rows_ref, shares, gram_ref = refs[:count], refs[count], refs[count + 1 : -1], refs[-1]
    years, _, rank = rows_ref.shape
    half = rank // 2
    for y in range(years):
        total = parts[0][y]
        for part in parts[1:]:
            total += part[y].astype(F32)
        rows = total.astype(rows_ref.dtype)
        rows_ref[y] = rows
        gram = dot(rows, rows, ((0,), (0,)))
        first = 3 * half * y
        gram_ref[first : first + half, :] = gram[:half, :half]
        gram_ref[first + half : first + 2 * half, :] = gram[:half, half:]
        gram_ref[first + 2 * half : first + 3 * half, :] = gram[half:, half:]
    words, height, _ = shares[0].shape
    for shift, share in enumerate(shares):
        owner = lax.rem(me_ref[0] + shift, count)
        for w in range(words):
            at = pl.multiple_of((owner * words + w) * height, height)
            share[w] = gram_ref[pl.ds(at, height), :]


def rows_and_gram(me, parts, words):
    count = len(parts)
    years, _, rank = parts[0].shape
    gram_rows = 3 * years * rank // 2
    share = jax.ShapeDtypeStruct((words, gram_rows // (count * words), rank // 2), F32)
    return pl.pallas_call(
        rows_kernel,
        in_specs=[SMEM_SPEC] + [VMEM_SPEC] * count,
        out_specs=[VMEM_SPEC] * (1 + count),
        out_shape=[jax.ShapeDtypeStruct(parts[0].shape, BF16)] + [share] * count,
        scratch_shapes=[pltpu.VMEM((gram_rows, rank // 2), F32)],
        compiler_params=params(),
        name="rows_and_gram",
    )(me, *parts)


def spread_kernel(parts_ref, *refs):
    out_ref = refs[-1]
    total = parts_ref[0]
    for i in range(1, parts_ref.shape[0]):
        total += parts_ref[i]
    for w in range(out_ref.shape[0]):
        out_ref[w] = total


def spread_sum(parts, copies, *after):
    return pl.pallas_call(
        spread_kernel,
        in_specs=[VMEM_SPEC] + [ANY_SPEC] * len(after),
        out_specs=VMEM_SPEC,
        out_shape=jax.ShapeDtypeStruct((copies,) + parts.shape[1:], F32),
        compiler_params=params(),
        name="spread_sum",
    )(parts, *after)


NEWTON_MOST = 48
NEWTON_SETTLED = 4e-8


def identity(size):
    rows = lax.broadcasted_iota(jnp.int32, (size, size), 0)
    return jnp.where(rows == lax.broadcasted_iota(jnp.int32, (size, size), 1), 1.0, 0.0)


def inverses(grams, scaled_ref, guess_ref, rest_ref):
    count, size = len(grams), grams[0].shape[0]
    eye = identity(size)
    scales = []

    def residual():
        most = None
        for b in range(count):
            rest = eye - exact(scaled_ref[b], guess_ref[b])
            rest_ref[b] = rest
            square = jnp.sum(rest * rest)
            most = square if most is None else jnp.maximum(most, square)
        return most

    def improve():
        for b in range(count):
            guess = guess_ref[b]
            guess_ref[b] = guess + close(halves(guess), halves(rest_ref[b]))

    for b, gram in enumerate(grams):
        diagonal = gram * eye
        across = lax.rsqrt(jnp.sum(diagonal, axis=0, keepdims=True))
        down = lax.rsqrt(jnp.sum(diagonal, axis=1, keepdims=True))
        scaled = gram * across * down
        bound = jnp.max(jnp.sum(jnp.abs(scaled), axis=0, keepdims=True), axis=1, keepdims=True)
        scaled_ref[b] = scaled
        guess_ref[b] = eye / bound
        scales.append((across, down))

    def step(state):
        improve()
        return state[0] + 1, residual()

    lax.while_loop(
        lambda state: (state[0] < NEWTON_MOST) & (state[1] > NEWTON_SETTLED), step, (0, residual())
    )
    improve()
    return [guess_ref[b] * across * down for b, (across, down) in enumerate(scales)]


def newton_scratch(count, rank):
    return [pltpu.VMEM((count, rank, rank), F32)] * 3


def context_inverse_kernel(after_ref, mixing_ref, weights_ref, inverse_ref, *scratch):
    mixing_gram = exact(mixing_ref[...], mixing_ref[...], ((0,), (0,)))
    weight_gram = exact(weights_ref[...], weights_ref[...], ((0,), (0,)))
    (inverse,) = inverses([mixing_gram * weight_gram], *scratch)
    inverse_ref[...] = inverse


def context_inverse(after, mixing, year_weights):
    return pl.pallas_call(
        context_inverse_kernel,
        in_specs=[ANY_SPEC] + [VMEM_SPEC] * 2,
        out_specs=VMEM_SPEC,
        out_shape=jax.ShapeDtypeStruct(mixing.shape, F32),
        scratch_shapes=newton_scratch(1, mixing.shape[0]),
        compiler_params=params(),
        name="context_inverse",
    )(after, mixing, year_weights)


def frames_kernel(parts, at_ref, slices_ref, *refs):
    refs = refs[parts - 1 :]
    grams, rows = refs[:parts], refs[parts : 2 * parts]
    coupled_ref, weighted_ref, weights_ref, mixing_ref = refs[2 * parts : 2 * parts + 4]
    keep_ref, give_ref, side_keep_ref, side_give_ref = refs[2 * parts + 4 : 2 * parts + 8]
    tile_ref, packed_ref, gram_ref, rows_ref, lifted_ref, side_ref, sem = refs[2 * parts + 8 :]
    years, tile_rows, columns = tile_ref.shape
    rank = mixing_ref.shape[0]
    load = pltpu.make_async_copy(slices_ref, tile_ref, sem)
    load.start()
    me, core, year_first = at_ref[0], at_ref[1], at_ref[2]
    words, share, _ = grams[0].shape
    chunk = rows[0].shape[1]
    for shift in range(parts):
        owner = lax.rem(me + (parts - shift), parts)
        for w in range(words):
            at = pl.multiple_of((owner * words + w) * share, share)
            packed_ref[pl.ds(at, share), :] = grams[shift][w]
        for y in range(years):
            at = pl.multiple_of(owner * chunk, chunk)
            rows_ref[y, pl.ds(at, chunk), :] = rows[shift][y]
    edge = rank // 2
    for y in range(years):
        first = 3 * edge * y
        cross = packed_ref[first + edge : first + 2 * edge, :]
        gram_ref[y, :edge, :edge] = packed_ref[first : first + edge, :]
        gram_ref[y, :edge, edge:] = cross
        gram_ref[y, edge:, :edge] = cross.T
        gram_ref[y, edge:, edge:] = packed_ref[first + 2 * edge : first + 3 * edge, :]

    row_at = lax.broadcasted_iota(jnp.int32, (rank, rank), 0)
    diagonal = row_at == lax.broadcasted_iota(jnp.int32, (rank, rank), 1)
    coupled = [coupled_ref[y] for y in range(years)]
    half_way = [sum(dot(coupled[y], p, ((0,), (0,))) for p in thirds(gram_ref[y])) for y in range(years)]
    squares = [sum(dot(p, coupled[y]) for p in thirds(half_way[y])) for y in range(years)]
    traces = [
        jnp.sum(jnp.sum(jnp.where(diagonal, s, 0.0), axis=1, keepdims=True), axis=0, keepdims=True) + 1e-06
        for s in squares
    ]
    gram_now = [squares[y] / traces[y] for y in range(years)]
    polar = [None] * years
    for sweep in range(NS_STEPS):
        factor = [jnp.where(diagonal, 1.5, 0.0) - 0.5 * g for g in gram_now]
        split = [halves(f) for f in factor]
        polar = [factor[y] if sweep == 0 else close(halves(polar[y]), split[y]) for y in range(years)]
        if sweep < NS_STEPS - 1:
            gram_now = [close(halves(gram_now[y]), split[y]) for y in range(years)]
            gram_now = [close(halves(gram_now[y]), split[y]) for y in range(years)]
    scale = [lax.rsqrt(t) for t in traces]
    lift = [sum(dot(p, weighted_ref[y]) for p in halves(polar[y])) for y in range(years)]
    lift = [sum(dot(coupled[y], p) for p in halves(lift[y])) * scale[y] for y in range(years)]
    side_ref[rank:, :] = jnp.zeros((side_ref.shape[0] - rank, rank), F32)
    mixing_part = None
    for y in range(years):
        through = close(halves(polar[y]), halves(half_way[y]), ((0,), (0,))) * scale[y]
        term = weights_ref[pl.ds(year_first + y, 1), :] * through
        mixing_part = term if mixing_part is None else mixing_part + term
        side_ref[pl.ds(rank + year_first + y, 1), :] = jnp.sum(
            mixing_ref[...] * through, axis=0, keepdims=True
        )
    side_ref[:rank, :] = mixing_part
    half_years = (side_ref.shape[0] - rank) // 2
    for target, side in ((side_keep_ref, core), (side_give_ref, 1 - core)):
        target[:edge, :] = side_ref[pl.ds(pl.multiple_of(side * edge, edge), edge), :]
        target[edge:, :] = side_ref[pl.ds(pl.multiple_of(rank + side * half_years, half_years), half_years), :]
    for y in range(years):
        high, low = halves(lift[y])
        lifted = dot(high, rows_ref[y], ((0,), (1,))) + dot(low, rows_ref[y], ((0,), (1,)))
        lifted_ref[:, y * tile_rows : (y + 1) * tile_rows] = lifted.astype(BF16)
    load.wait()
    half = columns // 2
    width = rank
    for target, side in ((give_ref, 1 - core), (keep_ref, core)):
        for first in range(0, half, width):
            at = pl.multiple_of(side * half + first, width)
            total = dot(lifted_ref[:, :tile_rows], tile_ref[0, :, pl.ds(at, width)])
            for y in range(1, years):
                total += dot(
                    lifted_ref[:, y * tile_rows : (y + 1) * tile_rows], tile_ref[y, :, pl.ds(at, width)]
                )
            target[first : first + width, :] = total.T.astype(target.dtype)


def frames_and_context(at, slices, after, grams, rows, coupled, weighted, year_weights, mixing):
    parts = len(grams)
    years, tile_rows, columns = slices.shape
    rank = mixing.shape[0]
    side_rows = rank + year_weights.shape[0]
    return pl.pallas_call(
        functools.partial(frames_kernel, parts),
        in_specs=[SMEM_SPEC, ANY_SPEC] + [ANY_SPEC] * len(after) + [VMEM_SPEC] * (2 * parts + 4),
        out_specs=[VMEM_SPEC] * 4,
        out_shape=[
            jax.ShapeDtypeStruct((columns // 2, rank), F32),
            jax.ShapeDtypeStruct((columns // 2, rank), BF16),
            jax.ShapeDtypeStruct((side_rows // 2, rank), F32),
            jax.ShapeDtypeStruct((side_rows // 2, rank), F32),
        ],
        scratch_shapes=[
            pltpu.VMEM((years, tile_rows, columns), BF16),
            pltpu.VMEM((3 * years * rank // 2, rank // 2), F32),
            pltpu.VMEM((years, rank, rank), F32),
            pltpu.VMEM((years, tile_rows, rank), BF16),
            pltpu.VMEM((rank, years * tile_rows), BF16),
            pltpu.VMEM((side_rows, rank), F32),
            pltpu.SemaphoreType.DMA(()),
        ],
        compiler_params=params(),
        name="frames_and_context",
    )(at, slices, *after, *grams, *rows, coupled, weighted, year_weights, mixing)


SCALE_ROWS = 8


def pack_kernel(parts_ref, inverse_ref, *refs):
    packed_ref = refs[-1]
    count, height, rank = parts_ref.shape
    total = parts_ref[0].astype(F32)
    for i in range(1, count):
        total += parts_ref[i].astype(F32)
    total = exact(total, inverse_ref[...])
    most = jnp.max(jnp.max(jnp.abs(total), axis=1, keepdims=True), axis=0, keepdims=True)
    power = jnp.clip(jnp.ceil(jnp.log2(most)), -120.0, 120.0)
    total = total * jnp.exp2(-power)
    packed_ref[:height, :] = total[:, : rank // 2]
    packed_ref[height : 2 * height, :] = total[:, rank // 2 :]
    packed_ref[2 * height :, :] = jnp.broadcast_to(power, (SCALE_ROWS, rank // 2))


def pack_sum(parts, inverse, *after):
    _, height, rank = parts.shape
    return pl.pallas_call(
        pack_kernel,
        in_specs=[VMEM_SPEC] * 2 + [ANY_SPEC] * len(after),
        out_specs=VMEM_SPEC,
        out_shape=jax.ShapeDtypeStruct((2 * height + SCALE_ROWS, rank // 2), F32),
        compiler_params=params(),
        name="pack_sum",
    )(parts, inverse, *after)


def sum_kernel(*refs):
    total = refs[0][...]
    for ref in refs[1:-1]:
        total += ref[...]
    refs[-1][...] = total


def sum_all(values):
    return pl.pallas_call(
        sum_kernel,
        in_specs=[VMEM_SPEC] * len(values),
        out_specs=VMEM_SPEC,
        out_shape=jax.ShapeDtypeStruct(values[0].shape, values[0].dtype),
        compiler_params=params(),
        name="sum_all",
    )(*values)


def solve_kernel(parts, core_ref, after_ref, mixing_ref, weights_ref, mine_ref, other_ref, *refs):
    sides, (out_ref, gram_ref), scratch = refs[:parts], refs[parts : parts + 2], refs[parts + 2 :]
    edge = mine_ref.shape[0]
    for piece, side in ((mine_ref, core_ref[0]), (other_ref, 1 - core_ref[0])):
        gram_ref[pl.ds(pl.multiple_of(side * edge, edge), edge), :] = piece[...]
    mixing_gram = exact(mixing_ref[...], mixing_ref[...], ((0,), (0,)))
    weight_gram = exact(weights_ref[...], weights_ref[...], ((0,), (0,)))
    factor_gram = gram_ref[...]
    first, second = inverses([factor_gram * weight_gram, mixing_gram * factor_gram], *scratch)
    side = sides[0][...]
    for piece in sides[1:]:
        side += piece[...]
    out_ref[:edge, :] = exact(side[:edge], first)
    out_ref[edge:, :] = exact(side[edge:], second)


def solve_sides(core, after, mixing, year_weights, mine, other, sides):
    rank = mixing.shape[0]
    return pl.pallas_call(
        functools.partial(solve_kernel, len(sides)),
        in_specs=[SMEM_SPEC, ANY_SPEC] + [VMEM_SPEC] * (4 + len(sides)),
        out_specs=VMEM_SPEC,
        out_shape=jax.ShapeDtypeStruct(sides[0].shape, F32),
        scratch_shapes=[pltpu.VMEM((rank, rank), F32)] + newton_scratch(2, rank),
        compiler_params=params(),
        name="solve_sides",
    )(core, after, mixing, year_weights, mine, other, *sides)


def unpack_kernel(core_ref, mine_ref, other_ref, out_ref):
    count, height, width = mine_ref.shape
    height = (height - SCALE_ROWS) // 2
    for ref, side in ((mine_ref, core_ref[0]), (other_ref, 1 - core_ref[0])):
        for i in range(count):
            value = ref[i]
            scale = jnp.exp2(value[2 * height : 2 * height + 1, :])
            at = pl.ds(pl.multiple_of((side * count + i) * height, height), height)
            out_ref[at, :width] = value[:height] * scale
            out_ref[at, width:] = value[height : 2 * height] * scale


def unpack(core, mine, other):
    count, height, width = mine.shape
    rows = 2 * count * ((height - SCALE_ROWS) // 2)
    return pl.pallas_call(
        unpack_kernel,
        in_specs=[SMEM_SPEC, VMEM_SPEC, VMEM_SPEC],
        out_specs=VMEM_SPEC,
        out_shape=jax.ShapeDtypeStruct((rows, 2 * width), F32),
        compiler_params=params(),
        name="unpack",
    )(core, mine, other)


def around(value, axis):
    size = lax.axis_size(axis)
    return [value] + [
        lax.ppermute(value, axis, [(i, (i + shift) % size) for i in range(size)]) for shift in range(1, size)
    ]


def in_order(core, mine, other):
    return [jnp.where(core == 0, mine, other), jnp.where(core == 0, other, mine)]


def local(slices, context_factor, mixing, year_weights):
    years_here = slices.shape[0]
    rank = mixing.shape[0]
    x_count, cores = lax.axis_size("x"), lax.axis_size("core")
    word_count, parts = lax.axis_size("word"), lax.axis_size("context")
    x_me, core, me = lax.axis_index("x"), lax.axis_index("core"), lax.axis_index("context")
    year_first = (x_me * cores + core) * years_here
    at = jnp.stack([me, core, year_first]).astype(jnp.int32)
    local_weights = lax.dynamic_slice_in_dim(year_weights, year_first, years_here, 0)
    coupled = (local_weights[:, :, None] * mixing.T[None, :, :]).astype(BF16)
    weighted = (mixing[None, :, :] * local_weights[:, None, :]).astype(BF16)

    me_at, core_at = at[:1], core.astype(jnp.int32)[None]

    def send(value, shift):
        return lax.ppermute(value, "context", [(i, (i + shift) % parts) for i in range(parts)])

    middle = parts // 2
    order = ((middle, 1, 1), (1, middle, 2))
    arrived = []
    for shifts in order:
        sent = reduced_parts(slices, context_factor, me_at, parts, shifts, BF16)
        arrived += [send(value, shifts[0] + shifts[1] * i) for i, value in enumerate(sent)]
    (own,) = reduced_parts(slices, context_factor, me_at, parts, (0, 1, 1), F32)
    own_rows, *shares = rows_and_gram(me_at, [own] + arrived, word_count)
    gram_part = sum_all([shares[0]] + [send(shares[shift], shift) for shift in range(1, parts)])
    gram_part = lax.all_to_all(gram_part, "word", 0, 0, tiled=True)
    rows = around(own_rows, "context")
    spread = spread_sum(gram_part, word_count, *rows[1:])
    factor_parts = around(factor_share(core_at, spread, context_factor, cores), "context")
    grams = around(lax.all_to_all(spread, "word", 0, 0, tiled=True), "context")

    keep, give, side_keep, side_give = frames_and_context(
        at, slices, factor_parts[1:], grams, rows, coupled, weighted, year_weights, mixing
    )

    swap = [(i, cores - 1 - i) for i in range(cores)]
    count = x_count * word_count
    both = (keep + lax.ppermute(give, "core", swap).astype(F32)).astype(BF16).reshape(count, -1, rank)
    sides = around(side_keep + lax.ppermute(side_give, "core", swap), "x")
    factor_half = sum_all(factor_parts)
    factor_other = lax.ppermute(factor_half, "core", swap)
    both_parts = lax.all_to_all(both, ("x", "word"), 0, 0, tiled=True)
    inverse = context_inverse(both, mixing, year_weights)
    packed = pack_sum(both_parts, inverse, factor_other, *sides[1:])
    spread = jnp.broadcast_to(packed.astype(jnp.float16)[None], (count,) + packed.shape)
    mine = lax.all_to_all(spread, ("x", "word"), 0, 0, tiled=True)
    solved = solve_sides(core_at, packed, mixing, year_weights, factor_half, factor_other, sides)
    solved = in_order(core, solved, lax.ppermute(solved, "core", swap))
    edge = rank // 2
    new_mixing = jnp.concatenate([solved[0][:edge], solved[1][:edge]])
    new_years = jnp.concatenate([solved[0][edge:], solved[1][edge:]])
    other = lax.ppermute(mine, "core", swap)
    new_context = unpack(core_at, mine.astype(F32), other.astype(F32))
    return (new_mixing, new_context, new_years)


def solution(mesh):
    year_count, word_count, context_count = mesh.devices.shape
    cores = 2
    fine = Mesh(
        mesh.devices.reshape(year_count // cores, cores, word_count, context_count),
        ("x", "core", "word", "context"),
    )
    in_specs = (P(("x", "core"), "word", "context"), P("context", None), P(), P())
    out_specs = (P(), P("context", None), P())
    return jax.shard_map(local, mesh=fine, in_specs=in_specs, out_specs=out_specs, check_vma=False)
```

```python
import functools

import jax
import jax.numpy as jnp
from jax import lax
from jax.experimental import pallas as pl
from jax.experimental.pallas import tpu as pltpu
from jax.sharding import Mesh, PartitionSpec as P

NS_STEPS = 8
F32, BF16 = jnp.float32, jnp.bfloat16
HIGHEST = lax.Precision.HIGHEST
VMEM_BYTES = 48 * 1024 * 1024
VMEM_SPEC = pl.BlockSpec(memory_space=pltpu.VMEM)
SMEM_SPEC = pl.BlockSpec(memory_space=pltpu.SMEM)
ANY_SPEC = pl.BlockSpec(memory_space=pl.ANY)


def dot(a, b, contract=((1,), (0,)), precision=None):
    return lax.dot_general(a, b, (contract, ((), ())), precision=precision, preferred_element_type=F32)


def exact(a, b, contract=((1,), (0,))):
    return dot(a, b, contract, HIGHEST)


def halves(a):
    high = a.astype(BF16)
    return high, (a - high.astype(F32)).astype(BF16)


def thirds(a):
    high, rest = halves(a)
    return high, rest, (a - high.astype(F32) - rest.astype(F32)).astype(BF16)


def close(a, b, contract=((1,), (0,))):
    return dot(a[0], b[0], contract) + (dot(a[0], b[1], contract) + dot(a[1], b[0], contract))


def params():
    return pltpu.CompilerParams(vmem_limit_bytes=VMEM_BYTES)


def reduced_kernel(count, me_ref, slices_ref, factor_ref, *out_refs):
    step, y = pl.program_id(0), pl.program_id(1)
    product = dot(slices_ref[0], factor_ref[...])
    for i in range(count):

        @pl.when(step == i)
        def _():
            out_refs[i][y] = product.astype(out_refs[i].dtype)


def reduced_parts(slices, context_factor, me, parts, shifts, dtype):
    first, stride, count = shifts
    years, rows, columns = slices.shape
    rank = context_factor.shape[1]
    chunk = rows // parts
    out_block = pl.BlockSpec((years, chunk, rank), lambda s, y, m: (0, 0, 0))
    return pl.pallas_call(
        functools.partial(reduced_kernel, count),
        grid_spec=pltpu.PrefetchScalarGridSpec(
            num_scalar_prefetch=1,
            grid=(count, years),
            in_specs=[
                pl.BlockSpec(
                    (1, chunk, columns), lambda s, y, m: (y, lax.rem(m[0] + first + s * stride, parts), 0)
                ),
                pl.BlockSpec((columns, rank), lambda s, y, m: (0, 0)),
            ],
            out_specs=[out_block] * count,
        ),
        out_shape=[jax.ShapeDtypeStruct((years, chunk, rank), dtype)] * count,
        compiler_params=params(),
        name="reduced_parts",
    )(me, slices, context_factor)


def factor_share_kernel(at_ref, after_ref, factor_ref, out_ref, scratch):
    share = out_ref.shape[0]
    scratch[...] = dot(factor_ref[...], factor_ref[...], ((0,), (0,)))
    out_ref[...] = scratch[pl.ds(pl.multiple_of(at_ref[0] * share, share), share), :]


def factor_share(me, after, context_factor, shares):
    rank = context_factor.shape[1]
    return pl.pallas_call(
        factor_share_kernel,
        in_specs=[SMEM_SPEC, ANY_SPEC, VMEM_SPEC],
        out_specs=VMEM_SPEC,
        out_shape=jax.ShapeDtypeStruct((rank // shares, rank), F32),
        scratch_shapes=[pltpu.VMEM((rank, rank), F32)],
        compiler_params=params(),
        name="factor_share",
    )(me, after, context_factor)


def rows_kernel(me_ref, after_ref, *refs):
    count = (len(refs) - 2) // 2
    parts, rows_ref, shares, gram_ref = refs[:count], refs[count], refs[count + 1 : -1], refs[-1]
    years, _, rank = rows_ref.shape
    half = rank // 2
    for y in range(years):
        total = parts[0][y]
        for part in parts[1:]:
            total += part[y].astype(F32)
        rows = total.astype(rows_ref.dtype)
        rows_ref[y] = rows
        gram = dot(rows, rows, ((0,), (0,)))
        first = 3 * half * y
        gram_ref[first : first + half, :] = gram[:half, :half]
        gram_ref[first + half : first + 2 * half, :] = gram[:half, half:]
        gram_ref[first + 2 * half : first + 3 * half, :] = gram[half:, half:]
    words, height, _ = shares[0].shape
    for shift, share in enumerate(shares):
        owner = lax.rem(me_ref[0] + shift, count)
        for w in range(words):
            at = pl.multiple_of((owner * words + w) * height, height)
            share[w] = gram_ref[pl.ds(at, height), :]


def rows_and_gram(me, after, parts, words):
    count = len(parts)
    years, _, rank = parts[0].shape
    gram_rows = 3 * years * rank // 2
    share = jax.ShapeDtypeStruct((words, gram_rows // (count * words), rank // 2), F32)
    return pl.pallas_call(
        rows_kernel,
        in_specs=[SMEM_SPEC, ANY_SPEC] + [VMEM_SPEC] * count,
        out_specs=[VMEM_SPEC] * (1 + count),
        out_shape=[jax.ShapeDtypeStruct(parts[0].shape, BF16)] + [share] * count,
        scratch_shapes=[pltpu.VMEM((gram_rows, rank // 2), F32)],
        compiler_params=params(),
        name="rows_and_gram",
    )(me, after, *parts)


NEWTON_ROUGH = 4
NEWTON_MOST = 48
NEWTON_SETTLED = 4e-8


def identity(size):
    rows = lax.broadcasted_iota(jnp.int32, (size, size), 0)
    return jnp.where(rows == lax.broadcasted_iota(jnp.int32, (size, size), 1), 1.0, 0.0)


def inverses(grams, scaled_ref, guess_ref):
    count, size = len(grams), grams[0].shape[0]
    eye = identity(size)
    scales = []
    for b, gram in enumerate(grams):
        diagonal = gram * eye
        across = lax.rsqrt(jnp.sum(diagonal, axis=0, keepdims=True))
        down = lax.rsqrt(jnp.sum(diagonal, axis=1, keepdims=True))
        scaled = gram * across * down
        bound = jnp.max(jnp.sum(jnp.abs(scaled), axis=0, keepdims=True), axis=1, keepdims=True)
        scaled_ref[b] = scaled
        guess_ref[b] = (2.0 * eye - scaled / bound) / bound
        scales.append((across, down))

    def rough(_, carry):
        for b in range(count):
            guess = guess_ref[b].astype(BF16)
            rest = eye - dot(scaled_ref[b].astype(BF16), guess)
            guess_ref[b] = guess_ref[b] + dot(guess, rest.astype(BF16))
        return carry

    def step(state):
        most = None
        for b in range(count):
            guess = guess_ref[b]
            rest = eye - exact(scaled_ref[b], guess)
            guess_ref[b] = guess + close(halves(guess), halves(rest))
            square = jnp.sum(rest * rest)
            most = square if most is None else jnp.maximum(most, square)
        return state[0] + 1, most

    lax.fori_loop(0, NEWTON_ROUGH, rough, 0)
    lax.while_loop(
        lambda state: (state[0] < NEWTON_MOST) & (state[1] > NEWTON_SETTLED), step, (0, jnp.float32(1.0))
    )
    return [guess_ref[b] * across * down for b, (across, down) in enumerate(scales)]


def newton_scratch(count, rank):
    return [pltpu.VMEM((count, rank, rank), F32)] * 2


def context_inverse_kernel(after_ref, mixing_ref, weights_ref, inverse_ref, first_ref, second_ref, *scratch):
    first_ref[...] = exact(mixing_ref[...], mixing_ref[...], ((0,), (0,)))
    second_ref[...] = exact(weights_ref[...], weights_ref[...], ((0,), (0,)))
    (inverse,) = inverses([first_ref[...] * second_ref[...]], *scratch)
    inverse_ref[...] = inverse


def context_inverse(after, mixing, year_weights):
    return pl.pallas_call(
        context_inverse_kernel,
        in_specs=[ANY_SPEC] + [VMEM_SPEC] * 2,
        out_specs=[VMEM_SPEC] * 3,
        out_shape=[jax.ShapeDtypeStruct(mixing.shape, F32)] * 3,
        scratch_shapes=newton_scratch(1, mixing.shape[0]),
        compiler_params=params(),
        name="context_inverse",
    )(after, mixing, year_weights)


def frames_kernel(parts, at_ref, slices_ref, *refs):
    grams, rows = refs[:parts], refs[parts : 2 * parts]
    coupled_ref, weighted_ref, weights_ref, mixing_ref = refs[2 * parts : 2 * parts + 4]
    keep_ref, give_ref, side_keep_ref, side_give_ref = refs[2 * parts + 4 : 2 * parts + 8]
    tile_ref, packed_ref, gram_ref, half_ref, polar_ref, rows_ref, lifted_ref, side_ref, sem = refs[2 * parts + 8 :]
    years, tile_rows, columns = tile_ref.shape
    rank = mixing_ref.shape[0]
    load = pltpu.make_async_copy(slices_ref, tile_ref, sem)
    load.start()
    me, core, year_first = at_ref[0], at_ref[1], at_ref[2]
    words, share, _ = grams[0].shape
    chunk = rows[0].shape[1]
    for shift in range(parts):
        owner = lax.rem(me + (parts - shift), parts)
        for w in range(words):
            at = pl.multiple_of((owner * words + w) * share, share)
            packed_ref[pl.ds(at, share), :] = grams[shift][w]
        for y in range(years):
            at = pl.multiple_of(owner * chunk, chunk)
            rows_ref[y, pl.ds(at, chunk), :] = rows[shift][y]
    edge = rank // 2
    for y in range(years):
        first = 3 * edge * y
        cross = packed_ref[first + edge : first + 2 * edge, :]
        gram_ref[y, :edge, :edge] = packed_ref[first : first + edge, :]
        gram_ref[y, :edge, edge:] = cross
        gram_ref[y, edge:, :edge] = cross.T
        gram_ref[y, edge:, edge:] = packed_ref[first + 2 * edge : first + 3 * edge, :]

    row_at = lax.broadcasted_iota(jnp.int32, (rank, rank), 0)
    diagonal = row_at == lax.broadcasted_iota(jnp.int32, (rank, rank), 1)
    coupled = [coupled_ref[y] for y in range(years)]
    half_way = [sum(dot(coupled[y], p, ((0,), (0,))) for p in thirds(gram_ref[y])) for y in range(years)]
    squares = [sum(dot(p, coupled[y]) for p in thirds(half_way[y])) for y in range(years)]
    traces = [
        jnp.sum(jnp.sum(jnp.where(diagonal, s, 0.0), axis=1, keepdims=True), axis=0, keepdims=True) + 1e-06
        for s in squares
    ]
    for y in range(years):
        gram_ref[y] = squares[y] / traces[y]
        half_ref[y] = half_way[y]
        polar_ref[y] = jnp.where(diagonal, 1.0, 0.0)

    def factor_of(y):
        return halves(jnp.where(diagonal, 1.5, 0.0) - 0.5 * gram_ref[y])

    def sweep(_, carry):
        factor = [factor_of(y) for y in range(years)]
        for y in range(years):
            polar_ref[y] = close(halves(polar_ref[y]), factor[y])
        gram = [close(halves(gram_ref[y]), factor[y]) for y in range(years)]
        gram = [close(halves(gram[y]), factor[y]) for y in range(years)]
        for y in range(years):
            gram_ref[y] = gram[y]
        return carry

    lax.fori_loop(0, NS_STEPS - 1, sweep, 0)
    polar = [close(halves(polar_ref[y]), factor_of(y)) for y in range(years)]
    scale = [lax.rsqrt(t) for t in traces]
    lift = [sum(dot(p, weighted_ref[y]) for p in halves(polar[y])) for y in range(years)]
    lift = [sum(dot(coupled[y], p) for p in halves(lift[y])) * scale[y] for y in range(years)]
    side_ref[rank:, :] = jnp.zeros((side_ref.shape[0] - rank, rank), F32)
    mixing_part = None
    for y in range(years):
        through = close(halves(polar[y]), halves(half_ref[y]), ((0,), (0,))) * scale[y]
        term = weights_ref[pl.ds(year_first + y, 1), :] * through
        mixing_part = term if mixing_part is None else mixing_part + term
        side_ref[pl.ds(rank + year_first + y, 1), :] = jnp.sum(
            mixing_ref[...] * through, axis=0, keepdims=True
        )
    side_ref[:rank, :] = mixing_part
    half_years = (side_ref.shape[0] - rank) // 2
    for target, side in ((side_keep_ref, core), (side_give_ref, 1 - core)):
        target[:edge, :] = side_ref[pl.ds(pl.multiple_of(side * edge, edge), edge), :]
        target[edge:, :] = side_ref[pl.ds(pl.multiple_of(rank + side * half_years, half_years), half_years), :]
    for y in range(years):
        high, low = halves(lift[y])
        lifted = dot(high, rows_ref[y], ((0,), (1,))) + dot(low, rows_ref[y], ((0,), (1,)))
        lifted_ref[:, y * tile_rows : (y + 1) * tile_rows] = lifted.astype(BF16)
    load.wait()
    half = columns // 2
    width = rank
    for target, side in ((give_ref, 1 - core), (keep_ref, core)):

        @pl.loop(0, half // width)
        def _(block):
            at = pl.multiple_of(side * half + block * width, width)
            total = dot(lifted_ref[:, :tile_rows], tile_ref[0, :, pl.ds(at, width)])
            for y in range(1, years):
                total += dot(
                    lifted_ref[:, y * tile_rows : (y + 1) * tile_rows], tile_ref[y, :, pl.ds(at, width)]
                )
            out_at = pl.ds(pl.multiple_of(block * width, width), width)
            target[out_at, :] = total.T.astype(target.dtype)


def frames_and_context(at, slices, grams, rows, coupled, weighted, year_weights, mixing):
    parts = len(grams)
    years, tile_rows, columns = slices.shape
    rank = mixing.shape[0]
    side_rows = rank + year_weights.shape[0]
    return pl.pallas_call(
        functools.partial(frames_kernel, parts),
        in_specs=[SMEM_SPEC, ANY_SPEC] + [VMEM_SPEC] * (2 * parts + 4),
        out_specs=[VMEM_SPEC] * 4,
        out_shape=[
            jax.ShapeDtypeStruct((columns // 2, rank), F32),
            jax.ShapeDtypeStruct((columns // 2, rank), BF16),
            jax.ShapeDtypeStruct((side_rows // 2, rank), F32),
            jax.ShapeDtypeStruct((side_rows // 2, rank), F32),
        ],
        scratch_shapes=[
            pltpu.VMEM((years, tile_rows, columns), BF16),
            pltpu.VMEM((3 * years * rank // 2, rank // 2), F32),
            pltpu.VMEM((years, rank, rank), F32),
            pltpu.VMEM((years, rank, rank), F32),
            pltpu.VMEM((years, rank, rank), F32),
            pltpu.VMEM((years, tile_rows, rank), BF16),
            pltpu.VMEM((rank, years * tile_rows), BF16),
            pltpu.VMEM((side_rows, rank), F32),
            pltpu.SemaphoreType.DMA(()),
        ],
        compiler_params=params(),
        cost_estimate=pl.CostEstimate(
            flops=12_000_000_000, bytes_accessed=40_000_000, transcendentals=0
        ),
        name="frames_and_context",
    )(at, slices, *grams, *rows, coupled, weighted, year_weights, mixing)


SCALE_ROWS = 8


def pack_kernel(parts_ref, inverse_ref, *refs):
    packed_ref = refs[-1]
    count, height, rank = parts_ref.shape
    total = parts_ref[0].astype(F32)
    for i in range(1, count):
        total += parts_ref[i].astype(F32)
    total = exact(total, inverse_ref[...])
    most = jnp.max(jnp.max(jnp.abs(total), axis=1, keepdims=True), axis=0, keepdims=True)
    power = jnp.clip(jnp.ceil(jnp.log2(most)), -120.0, 120.0)
    total = total * jnp.exp2(-power)
    packed_ref[:height, :] = total[:, : rank // 2]
    packed_ref[height : 2 * height, :] = total[:, rank // 2 :]
    packed_ref[2 * height :, :] = jnp.broadcast_to(power, (SCALE_ROWS, rank // 2))


def pack_sum(parts, inverse, *after):
    _, height, rank = parts.shape
    return pl.pallas_call(
        pack_kernel,
        in_specs=[VMEM_SPEC] * 2 + [ANY_SPEC] * len(after),
        out_specs=VMEM_SPEC,
        out_shape=jax.ShapeDtypeStruct((2 * height + SCALE_ROWS, rank // 2), F32),
        compiler_params=params(),
        name="pack_sum",
    )(parts, inverse, *after)


def sum_kernel(count, *refs):
    total = refs[0][...]
    for ref in refs[1:count]:
        total += ref[...]
    refs[-1][...] = total


def sum_all(values, *after):
    return pl.pallas_call(
        functools.partial(sum_kernel, len(values)),
        in_specs=[VMEM_SPEC] * len(values) + [ANY_SPEC] * len(after),
        out_specs=VMEM_SPEC,
        out_shape=jax.ShapeDtypeStruct(values[0].shape, values[0].dtype),
        compiler_params=params(),
        name="sum_all",
    )(*values, *after)


def add_cores_kernel(keep_ref, got_ref, out_ref):
    out_ref[...] = (keep_ref[...] + got_ref[...].astype(F32)).astype(out_ref.dtype)


def add_cores(keep, got):
    return pl.pallas_call(
        add_cores_kernel,
        in_specs=[VMEM_SPEC] * 2,
        out_specs=VMEM_SPEC,
        out_shape=jax.ShapeDtypeStruct(keep.shape, BF16),
        compiler_params=params(),
        name="add_cores",
    )(keep, got)


def factor_inverses_kernel(core_ref, after_ref, mixing_ref, weights_ref, mine_ref, other_ref, *refs):
    first_ref, second_ref, gram_ref = refs[:3]
    edge = mine_ref.shape[0]
    for piece, side in ((mine_ref, core_ref[0]), (other_ref, 1 - core_ref[0])):
        gram_ref[pl.ds(pl.multiple_of(side * edge, edge), edge), :] = piece[...]
    factor_gram = gram_ref[...]
    first, second = inverses([factor_gram * weights_ref[...], mixing_ref[...] * factor_gram], *refs[3:])
    first_ref[...] = first
    second_ref[...] = second


def factor_inverses(core, after, mixing_gram, weight_gram, mine, other):
    rank = mixing_gram.shape[0]
    return pl.pallas_call(
        factor_inverses_kernel,
        in_specs=[SMEM_SPEC, ANY_SPEC] + [VMEM_SPEC] * 4,
        out_specs=[VMEM_SPEC] * 2,
        out_shape=[jax.ShapeDtypeStruct((rank, rank), F32)] * 2,
        scratch_shapes=[pltpu.VMEM((rank, rank), F32)] + newton_scratch(2, rank),
        compiler_params=params(),
        name="factor_inverses",
    )(core, after, mixing_gram, weight_gram, mine, other)


def solve_kernel(after_ref, first_ref, second_ref, *refs):
    sides, out_ref = refs[:-1], refs[-1]
    side = sides[0][...]
    for piece in sides[1:]:
        side += piece[...]
    edge = first_ref.shape[0] // 2
    out_ref[:edge, :] = exact(side[:edge], first_ref[...])
    out_ref[edge:, :] = exact(side[edge:], second_ref[...])


def solve_sides(after, first_inverse, second_inverse, sides):
    return pl.pallas_call(
        solve_kernel,
        in_specs=[ANY_SPEC] + [VMEM_SPEC] * (2 + len(sides)),
        out_specs=VMEM_SPEC,
        out_shape=jax.ShapeDtypeStruct(sides[0].shape, F32),
        compiler_params=params(),
        name="solve_sides",
    )(after, first_inverse, second_inverse, *sides)


def unpack_kernel(core_ref, mine_ref, other_ref, out_ref):
    count, height, width = mine_ref.shape
    height = (height - SCALE_ROWS) // 2
    for ref, side in ((mine_ref, core_ref[0]), (other_ref, 1 - core_ref[0])):
        for i in range(count):
            value = ref[i]
            scale = jnp.exp2(value[2 * height : 2 * height + 1, :])
            at = pl.ds(pl.multiple_of((side * count + i) * height, height), height)
            out_ref[at, :width] = value[:height] * scale
            out_ref[at, width:] = value[height : 2 * height] * scale


def unpack(core, mine, other):
    count, height, width = mine.shape
    rows = 2 * count * ((height - SCALE_ROWS) // 2)
    return pl.pallas_call(
        unpack_kernel,
        in_specs=[SMEM_SPEC, VMEM_SPEC, VMEM_SPEC],
        out_specs=VMEM_SPEC,
        out_shape=jax.ShapeDtypeStruct((rows, 2 * width), F32),
        compiler_params=params(),
        name="unpack",
    )(core, mine, other)


def around(value, axis):
    size = lax.axis_size(axis)
    return [value] + [
        lax.ppermute(value, axis, [(i, (i + shift) % size) for i in range(size)]) for shift in range(1, size)
    ]


def in_order(core, mine, other):
    return [jnp.where(core == 0, mine, other), jnp.where(core == 0, other, mine)]


def local(slices, context_factor, mixing, year_weights):
    years_here = slices.shape[0]
    rank = mixing.shape[0]
    x_count, cores = lax.axis_size("x"), lax.axis_size("core")
    word_count, parts = lax.axis_size("word"), lax.axis_size("context")
    x_me, core, me = lax.axis_index("x"), lax.axis_index("core"), lax.axis_index("context")
    year_first = (x_me * cores + core) * years_here
    at = jnp.stack([me, core, year_first]).astype(jnp.int32)
    local_weights = lax.dynamic_slice_in_dim(year_weights, year_first, years_here, 0)
    coupled = (local_weights[:, :, None] * mixing.T[None, :, :]).astype(BF16)
    weighted = (mixing[None, :, :] * local_weights[:, None, :]).astype(BF16)

    me_at, core_at = at[:1], core.astype(jnp.int32)[None]

    def send(value, shift):
        return lax.ppermute(value, "context", [(i, (i + shift) % parts) for i in range(parts)])

    middle = parts // 2
    order = ((middle, 1, 1), (1, middle, 2))
    arrived = []
    for shifts in order:
        sent = reduced_parts(slices, context_factor, me_at, parts, shifts, BF16)
        arrived += [send(value, shifts[0] + shifts[1] * i) for i, value in enumerate(sent)]
    (own,) = reduced_parts(slices, context_factor, me_at, parts, (0, 1, 1), F32)
    inverse, mixing_gram, weight_gram = context_inverse(own, mixing, year_weights)
    own_rows, *shares = rows_and_gram(me_at, inverse, [own] + arrived, word_count)
    gram_part = sum_all([shares[0]] + [send(shares[shift], shift) for shift in range(1, parts)])
    rows = around(own_rows, "context")
    distance = 1
    while distance < word_count:
        got = lax.ppermute(gram_part, "word", [(i, i ^ distance) for i in range(word_count)])
        distance *= 2
        gram_part = sum_all([gram_part, got], *(rows[1:] if distance == word_count else []))
    grams = around(gram_part, "context")

    keep, give, side_keep, side_give = frames_and_context(
        at, slices, grams, rows, coupled, weighted, year_weights, mixing
    )

    swap = [(i, cores - 1 - i) for i in range(cores)]
    count = x_count * word_count
    both = add_cores(keep, lax.ppermute(give, "core", swap)).reshape(count, -1, rank)
    factor_half = sum_all(around(factor_share(core_at, both, context_factor, cores), "context"))
    factor_other = lax.ppermute(factor_half, "core", swap)
    side_got = lax.ppermute(side_give, "core", swap)
    both_parts = lax.all_to_all(both, ("x", "word"), 0, 0, tiled=True)
    packed = pack_sum(both_parts, inverse, factor_other, side_got)
    first, second = factor_inverses(core_at, packed, mixing_gram, weight_gram, factor_half, factor_other)
    spread = jnp.broadcast_to(packed.astype(jnp.float16)[None], (count,) + packed.shape)
    mine = lax.all_to_all(spread, ("x", "word"), 0, 0, tiled=True)
    sides = around(sum_all([side_keep, side_got], packed), "x")
    solved = solve_sides(packed, first, second, sides)
    solved = in_order(core, solved, lax.ppermute(solved, "core", swap))
    edge = rank // 2
    new_mixing = jnp.concatenate([solved[0][:edge], solved[1][:edge]])
    new_years = jnp.concatenate([solved[0][edge:], solved[1][edge:]])
    other = lax.ppermute(mine, "core", swap)
    new_context = unpack(core_at, mine.astype(F32), other.astype(F32))
    return (new_mixing, new_context, new_years)


def solution(mesh):
    year_count, word_count, context_count = mesh.devices.shape
    cores = 2
    fine = Mesh(
        mesh.devices.reshape(year_count // cores, cores, word_count, context_count),
        ("x", "core", "word", "context"),
    )
    in_specs = (P(("x", "core"), "word", "context"), P("context", None), P(), P())
    out_specs = (P(), P("context", None), P())
    return jax.shard_map(local, mesh=fine, in_specs=in_specs, out_specs=out_specs, check_vma=False)
```

```python
import functools

import jax
import jax.numpy as jnp
from jax import lax
from jax.experimental import pallas as pl
from jax.experimental.pallas import tpu as pltpu
from jax.sharding import Mesh, PartitionSpec as P

NS_STEPS = 8
F32, BF16 = jnp.float32, jnp.bfloat16
HIGHEST = lax.Precision.HIGHEST
VMEM_BYTES = 48 * 1024 * 1024
VMEM_SPEC = pl.BlockSpec(memory_space=pltpu.VMEM)
SMEM_SPEC = pl.BlockSpec(memory_space=pltpu.SMEM)
ANY_SPEC = pl.BlockSpec(memory_space=pl.ANY)


def dot(a, b, contract=((1,), (0,)), precision=None):
    return lax.dot_general(a, b, (contract, ((), ())), precision=precision, preferred_element_type=F32)


def exact(a, b, contract=((1,), (0,))):
    return dot(a, b, contract, HIGHEST)


def halves(a):
    high = a.astype(BF16)
    return high, (a - high.astype(F32)).astype(BF16)


def thirds(a):
    high, rest = halves(a)
    return high, rest, (a - high.astype(F32) - rest.astype(F32)).astype(BF16)


def close(a, b, contract=((1,), (0,))):
    return dot(a[0], b[0], contract) + (dot(a[0], b[1], contract) + dot(a[1], b[0], contract))


def close_each(left, b):
    split = [halves(a) for a in left]
    highs, lows = [a[0] for a in split], [a[1] for a in split]
    size = left[0].shape[0]
    by_high = dot(jnp.concatenate(highs + lows), b[0])
    by_low = dot(jnp.concatenate(highs), b[1])
    parts = [by_high[i * size : (i + 1) * size] for i in range(2 * len(left))]
    return [
        parts[i] + (by_low[i * size : (i + 1) * size] + parts[len(left) + i]) for i in range(len(left))
    ]


def params():
    return pltpu.CompilerParams(vmem_limit_bytes=VMEM_BYTES)


def reduced_kernel(count, me_ref, slices_ref, factor_ref, *out_refs):
    step, y = pl.program_id(0), pl.program_id(1)
    product = dot(slices_ref[0], factor_ref[...])
    for i in range(count):

        @pl.when(step == i)
        def _():
            out_refs[i][y] = product.astype(out_refs[i].dtype)


def reduced_parts(slices, context_factor, me, parts, shifts, dtype):
    first, stride, count = shifts
    years, rows, columns = slices.shape
    rank = context_factor.shape[1]
    chunk = rows // parts
    out_block = pl.BlockSpec((years, chunk, rank), lambda s, y, m: (0, 0, 0))
    return pl.pallas_call(
        functools.partial(reduced_kernel, count),
        grid_spec=pltpu.PrefetchScalarGridSpec(
            num_scalar_prefetch=1,
            grid=(count, years),
            in_specs=[
                pl.BlockSpec(
                    (1, chunk, columns), lambda s, y, m: (y, lax.rem(m[0] + first + s * stride, parts), 0)
                ),
                pl.BlockSpec((columns, rank), lambda s, y, m: (0, 0)),
            ],
            out_specs=[out_block] * count,
        ),
        out_shape=[jax.ShapeDtypeStruct((years, chunk, rank), dtype)] * count,
        compiler_params=params(),
        name="reduced_parts",
    )(me, slices, context_factor)


def factor_share_kernel(at_ref, after_ref, factor_ref, out_ref, scratch):
    share = out_ref.shape[0]
    scratch[...] = dot(factor_ref[...], factor_ref[...], ((0,), (0,)))
    out_ref[...] = scratch[pl.ds(pl.multiple_of(at_ref[0] * share, share), share), :]


def factor_share(me, after, context_factor, shares):
    rank = context_factor.shape[1]
    return pl.pallas_call(
        factor_share_kernel,
        in_specs=[SMEM_SPEC, ANY_SPEC, VMEM_SPEC],
        out_specs=VMEM_SPEC,
        out_shape=jax.ShapeDtypeStruct((rank // shares, rank), F32),
        scratch_shapes=[pltpu.VMEM((rank, rank), F32)],
        compiler_params=params(),
        name="factor_share",
    )(me, after, context_factor)


def rows_kernel(me_ref, after_ref, *refs):
    count = (len(refs) - 2) // 2
    parts, rows_ref, shares, gram_ref = refs[:count], refs[count], refs[count + 1 : -1], refs[-1]
    years, _, rank = rows_ref.shape
    half = rank // 2
    for y in range(years):
        total = parts[0][y]
        for part in parts[1:]:
            total += part[y].astype(F32)
        rows = total.astype(rows_ref.dtype)
        rows_ref[y] = rows
        gram = dot(rows, rows, ((0,), (0,)))
        first = 3 * half * y
        gram_ref[first : first + half, :] = gram[:half, :half]
        gram_ref[first + half : first + 2 * half, :] = gram[:half, half:]
        gram_ref[first + 2 * half : first + 3 * half, :] = gram[half:, half:]
    words, height, _ = shares[0].shape
    for shift, share in enumerate(shares):
        owner = lax.rem(me_ref[0] + shift, count)
        for w in range(words):
            at = pl.multiple_of((owner * words + w) * height, height)
            share[w] = gram_ref[pl.ds(at, height), :]


def rows_and_gram(me, after, parts, words):
    count = len(parts)
    years, _, rank = parts[0].shape
    gram_rows = 3 * years * rank // 2
    share = jax.ShapeDtypeStruct((words, gram_rows // (count * words), rank // 2), F32)
    return pl.pallas_call(
        rows_kernel,
        in_specs=[SMEM_SPEC, ANY_SPEC] + [VMEM_SPEC] * count,
        out_specs=[VMEM_SPEC] * (1 + count),
        out_shape=[jax.ShapeDtypeStruct(parts[0].shape, BF16)] + [share] * count,
        scratch_shapes=[pltpu.VMEM((gram_rows, rank // 2), F32)],
        compiler_params=params(),
        name="rows_and_gram",
    )(me, after, *parts)


NEWTON_ROUGH = 4
NEWTON_MOST = 48
NEWTON_SETTLED = 4e-8


def identity(size):
    rows = lax.broadcasted_iota(jnp.int32, (size, size), 0)
    return jnp.where(rows == lax.broadcasted_iota(jnp.int32, (size, size), 1), 1.0, 0.0)


def inverses(grams, scaled_ref, guess_ref):
    count, size = len(grams), grams[0].shape[0]
    eye = identity(size)
    scales = []
    for b, gram in enumerate(grams):
        diagonal = gram * eye
        across = lax.rsqrt(jnp.sum(diagonal, axis=0, keepdims=True))
        down = lax.rsqrt(jnp.sum(diagonal, axis=1, keepdims=True))
        scaled = gram * across * down
        bound = jnp.max(jnp.sum(jnp.abs(scaled), axis=0, keepdims=True), axis=1, keepdims=True)
        scaled_ref[b] = scaled
        guess_ref[b] = (2.0 * eye - scaled / bound) / bound
        scales.append((across, down))

    def rough(_, carry):
        for b in range(count):
            guess = guess_ref[b].astype(BF16)
            rest = eye - dot(scaled_ref[b].astype(BF16), guess)
            guess_ref[b] = guess_ref[b] + dot(guess, rest.astype(BF16))
        return carry

    def step(state):
        most = None
        for b in range(count):
            guess = guess_ref[b]
            rest = eye - exact(scaled_ref[b], guess)
            guess_ref[b] = guess + close(halves(guess), halves(rest))
            square = jnp.sum(rest * rest)
            most = square if most is None else jnp.maximum(most, square)
        return state[0] + 1, most

    lax.fori_loop(0, NEWTON_ROUGH, rough, 0)
    lax.while_loop(
        lambda state: (state[0] < NEWTON_MOST) & (state[1] > NEWTON_SETTLED), step, (0, jnp.float32(1.0))
    )
    return [guess_ref[b] * across * down for b, (across, down) in enumerate(scales)]


def newton_scratch(count, rank):
    return [pltpu.VMEM((count, rank, rank), F32)] * 2


def context_inverse_kernel(after_ref, mixing_ref, weights_ref, inverse_ref, first_ref, second_ref, *scratch):
    first_ref[...] = exact(mixing_ref[...], mixing_ref[...], ((0,), (0,)))
    second_ref[...] = exact(weights_ref[...], weights_ref[...], ((0,), (0,)))
    (inverse,) = inverses([first_ref[...] * second_ref[...]], *scratch)
    inverse_ref[...] = inverse


def context_inverse(after, mixing, year_weights):
    return pl.pallas_call(
        context_inverse_kernel,
        in_specs=[ANY_SPEC] + [VMEM_SPEC] * 2,
        out_specs=[VMEM_SPEC] * 3,
        out_shape=[jax.ShapeDtypeStruct(mixing.shape, F32)] * 3,
        scratch_shapes=newton_scratch(1, mixing.shape[0]),
        compiler_params=params(),
        name="context_inverse",
    )(after, mixing, year_weights)


def frames_kernel(parts, at_ref, slices_ref, *refs):
    grams, rows = refs[:parts], refs[parts : 2 * parts]
    coupled_ref, weighted_ref, weights_ref, mixing_ref = refs[2 * parts : 2 * parts + 4]
    keep_ref, give_ref, side_keep_ref, side_give_ref = refs[2 * parts + 4 : 2 * parts + 8]
    tile_ref, packed_ref, gram_ref, half_ref, polar_ref, rows_ref, lifted_ref, side_ref, sem = refs[2 * parts + 8 :]
    years, tile_rows, columns = tile_ref.shape
    rank = mixing_ref.shape[0]
    load = pltpu.make_async_copy(slices_ref, tile_ref, sem)
    load.start()
    me, core, year_first = at_ref[0], at_ref[1], at_ref[2]
    words, share, _ = grams[0].shape
    chunk = rows[0].shape[1]
    for shift in range(parts):
        owner = lax.rem(me + (parts - shift), parts)
        for w in range(words):
            at = pl.multiple_of((owner * words + w) * share, share)
            packed_ref[pl.ds(at, share), :] = grams[shift][w]
        for y in range(years):
            at = pl.multiple_of(owner * chunk, chunk)
            rows_ref[y, pl.ds(at, chunk), :] = rows[shift][y]
    edge = rank // 2
    for y in range(years):
        first = 3 * edge * y
        cross = packed_ref[first + edge : first + 2 * edge, :]
        gram_ref[y, :edge, :edge] = packed_ref[first : first + edge, :]
        gram_ref[y, :edge, edge:] = cross
        gram_ref[y, edge:, :edge] = cross.T
        gram_ref[y, edge:, edge:] = packed_ref[first + 2 * edge : first + 3 * edge, :]

    row_at = lax.broadcasted_iota(jnp.int32, (rank, rank), 0)
    diagonal = row_at == lax.broadcasted_iota(jnp.int32, (rank, rank), 1)
    coupled = [coupled_ref[y] for y in range(years)]
    half_way = [sum(dot(coupled[y], p, ((0,), (0,))) for p in thirds(gram_ref[y])) for y in range(years)]
    squares = [sum(dot(p, coupled[y]) for p in thirds(half_way[y])) for y in range(years)]
    traces = [
        jnp.sum(jnp.sum(jnp.where(diagonal, s, 0.0), axis=1, keepdims=True), axis=0, keepdims=True) + 1e-06
        for s in squares
    ]
    for y in range(years):
        gram_ref[y] = squares[y] / traces[y]
        half_ref[y] = half_way[y]
        polar_ref[y] = jnp.where(diagonal, 1.0, 0.0)

    def factor_of(y):
        return halves(jnp.where(diagonal, 1.5, 0.0) - 0.5 * gram_ref[y])

    def sweep(_, carry):
        factor = [factor_of(y) for y in range(years)]
        both = [close_each([gram_ref[y], polar_ref[y]], factor[y]) for y in range(years)]
        for y in range(years):
            polar_ref[y] = both[y][1]
        for y in range(years):
            gram_ref[y] = close_each([both[y][0]], factor[y])[0]
        return carry

    lax.fori_loop(0, NS_STEPS - 1, sweep, 0)
    polar = [close(halves(polar_ref[y]), factor_of(y)) for y in range(years)]
    scale = [lax.rsqrt(t) for t in traces]
    lift = [sum(dot(p, weighted_ref[y]) for p in halves(polar[y])) for y in range(years)]
    lift = [sum(dot(coupled[y], p) for p in halves(lift[y])) * scale[y] for y in range(years)]
    side_ref[rank:, :] = jnp.zeros((side_ref.shape[0] - rank, rank), F32)
    mixing_part = None
    for y in range(years):
        through = close(halves(polar[y]), halves(half_ref[y]), ((0,), (0,))) * scale[y]
        term = weights_ref[pl.ds(year_first + y, 1), :] * through
        mixing_part = term if mixing_part is None else mixing_part + term
        side_ref[pl.ds(rank + year_first + y, 1), :] = jnp.sum(
            mixing_ref[...] * through, axis=0, keepdims=True
        )
    side_ref[:rank, :] = mixing_part
    half_years = (side_ref.shape[0] - rank) // 2
    for target, side in ((side_keep_ref, core), (side_give_ref, 1 - core)):
        target[:edge, :] = side_ref[pl.ds(pl.multiple_of(side * edge, edge), edge), :]
        target[edge:, :] = side_ref[pl.ds(pl.multiple_of(rank + side * half_years, half_years), half_years), :]
    for y in range(years):
        high, low = halves(lift[y])
        lifted = dot(high, rows_ref[y], ((0,), (1,))) + dot(low, rows_ref[y], ((0,), (1,)))
        lifted_ref[:, y * tile_rows : (y + 1) * tile_rows] = lifted.astype(BF16)
    load.wait()
    half = columns // 2
    width = rank
    for target, side in ((give_ref, 1 - core), (keep_ref, core)):

        @pl.loop(0, half // width)
        def _(block):
            at = pl.multiple_of(side * half + block * width, width)
            total = dot(lifted_ref[:, :tile_rows], tile_ref[0, :, pl.ds(at, width)])
            for y in range(1, years):
                total += dot(
                    lifted_ref[:, y * tile_rows : (y + 1) * tile_rows], tile_ref[y, :, pl.ds(at, width)]
                )
            out_at = pl.ds(pl.multiple_of(block * width, width), width)
            target[out_at, :] = total.T.astype(target.dtype)


def frames_and_context(at, slices, grams, rows, coupled, weighted, year_weights, mixing):
    parts = len(grams)
    years, tile_rows, columns = slices.shape
    rank = mixing.shape[0]
    side_rows = rank + year_weights.shape[0]
    return pl.pallas_call(
        functools.partial(frames_kernel, parts),
        in_specs=[SMEM_SPEC, ANY_SPEC] + [VMEM_SPEC] * (2 * parts + 4),
        out_specs=[VMEM_SPEC] * 4,
        out_shape=[
            jax.ShapeDtypeStruct((columns // 2, rank), F32),
            jax.ShapeDtypeStruct((columns // 2, rank), BF16),
            jax.ShapeDtypeStruct((side_rows // 2, rank), F32),
            jax.ShapeDtypeStruct((side_rows // 2, rank), F32),
        ],
        scratch_shapes=[
            pltpu.VMEM((years, tile_rows, columns), BF16),
            pltpu.VMEM((3 * years * rank // 2, rank // 2), F32),
            pltpu.VMEM((years, rank, rank), F32),
            pltpu.VMEM((years, rank, rank), F32),
            pltpu.VMEM((years, rank, rank), F32),
            pltpu.VMEM((years, tile_rows, rank), BF16),
            pltpu.VMEM((rank, years * tile_rows), BF16),
            pltpu.VMEM((side_rows, rank), F32),
            pltpu.SemaphoreType.DMA(()),
        ],
        compiler_params=params(),
        cost_estimate=pl.CostEstimate(
            flops=12_000_000_000, bytes_accessed=40_000_000, transcendentals=0
        ),
        name="frames_and_context",
    )(at, slices, *grams, *rows, coupled, weighted, year_weights, mixing)


SCALE_ROWS = 8


def pack_kernel(parts_ref, inverse_ref, *refs):
    packed_ref = refs[-1]
    count, height, rank = parts_ref.shape
    total = parts_ref[0].astype(F32)
    for i in range(1, count):
        total += parts_ref[i].astype(F32)
    total = exact(total, inverse_ref[...])
    most = jnp.max(jnp.max(jnp.abs(total), axis=1, keepdims=True), axis=0, keepdims=True)
    power = jnp.clip(jnp.ceil(jnp.log2(most)), -120.0, 120.0)
    total = total * jnp.exp2(-power)
    packed_ref[:height, :] = total[:, : rank // 2]
    packed_ref[height : 2 * height, :] = total[:, rank // 2 :]
    packed_ref[2 * height :, :] = jnp.broadcast_to(power, (SCALE_ROWS, rank // 2))


def pack_sum(parts, inverse, *after):
    _, height, rank = parts.shape
    return pl.pallas_call(
        pack_kernel,
        in_specs=[VMEM_SPEC] * 2 + [ANY_SPEC] * len(after),
        out_specs=VMEM_SPEC,
        out_shape=jax.ShapeDtypeStruct((2 * height + SCALE_ROWS, rank // 2), F32),
        compiler_params=params(),
        name="pack_sum",
    )(parts, inverse, *after)


def sum_kernel(count, *refs):
    total = refs[0][...]
    for ref in refs[1:count]:
        total += ref[...]
    refs[-1][...] = total


def sum_all(values, *after):
    return pl.pallas_call(
        functools.partial(sum_kernel, len(values)),
        in_specs=[VMEM_SPEC] * len(values) + [ANY_SPEC] * len(after),
        out_specs=VMEM_SPEC,
        out_shape=jax.ShapeDtypeStruct(values[0].shape, values[0].dtype),
        compiler_params=params(),
        name="sum_all",
    )(*values, *after)


def add_cores_kernel(keep_ref, got_ref, out_ref):
    out_ref[...] = (keep_ref[...] + got_ref[...].astype(F32)).astype(out_ref.dtype)


def add_cores(keep, got):
    return pl.pallas_call(
        add_cores_kernel,
        in_specs=[VMEM_SPEC] * 2,
        out_specs=VMEM_SPEC,
        out_shape=jax.ShapeDtypeStruct(keep.shape, BF16),
        compiler_params=params(),
        name="add_cores",
    )(keep, got)


def factor_inverses_kernel(core_ref, after_ref, mixing_ref, weights_ref, mine_ref, other_ref, *refs):
    first_ref, second_ref, gram_ref = refs[:3]
    edge = mine_ref.shape[0]
    for piece, side in ((mine_ref, core_ref[0]), (other_ref, 1 - core_ref[0])):
        gram_ref[pl.ds(pl.multiple_of(side * edge, edge), edge), :] = piece[...]
    factor_gram = gram_ref[...]
    first, second = inverses([factor_gram * weights_ref[...], mixing_ref[...] * factor_gram], *refs[3:])
    first_ref[...] = first
    second_ref[...] = second


def factor_inverses(core, after, mixing_gram, weight_gram, mine, other):
    rank = mixing_gram.shape[0]
    return pl.pallas_call(
        factor_inverses_kernel,
        in_specs=[SMEM_SPEC, ANY_SPEC] + [VMEM_SPEC] * 4,
        out_specs=[VMEM_SPEC] * 2,
        out_shape=[jax.ShapeDtypeStruct((rank, rank), F32)] * 2,
        scratch_shapes=[pltpu.VMEM((rank, rank), F32)] + newton_scratch(2, rank),
        compiler_params=params(),
        name="factor_inverses",
    )(core, after, mixing_gram, weight_gram, mine, other)


def solve_kernel(after_ref, first_ref, second_ref, *refs):
    sides, out_ref = refs[:-1], refs[-1]
    side = sides[0][...]
    for piece in sides[1:]:
        side += piece[...]
    edge = first_ref.shape[0] // 2
    out_ref[:edge, :] = exact(side[:edge], first_ref[...])
    out_ref[edge:, :] = exact(side[edge:], second_ref[...])


def solve_sides(after, first_inverse, second_inverse, sides):
    return pl.pallas_call(
        solve_kernel,
        in_specs=[ANY_SPEC] + [VMEM_SPEC] * (2 + len(sides)),
        out_specs=VMEM_SPEC,
        out_shape=jax.ShapeDtypeStruct(sides[0].shape, F32),
        compiler_params=params(),
        name="solve_sides",
    )(after, first_inverse, second_inverse, *sides)


def unpack_kernel(side_ref, value_ref, *refs):
    out_ref = refs[-1]
    count, height, width = value_ref.shape
    height = (height - SCALE_ROWS) // 2
    for i in range(count):
        value = value_ref[i]
        scale = jnp.exp2(value[2 * height : 2 * height + 1, :])
        at = pl.ds(i * height, height)
        out_ref[at, :width] = value[:height] * scale
        out_ref[at, width:] = value[height : 2 * height] * scale


def unpack_into(side, value, out):
    count, height, width = value.shape
    rows = count * ((height - SCALE_ROWS) // 2)
    shape = jax.ShapeDtypeStruct((2 * rows, 2 * width), F32)
    whole = pl.BlockSpec(value.shape, lambda i, at: (0, 0, 0))
    return pl.pallas_call(
        unpack_kernel,
        grid_spec=pltpu.PrefetchScalarGridSpec(
            num_scalar_prefetch=1,
            grid=(1,),
            in_specs=[whole] + ([] if out is None else [ANY_SPEC]),
            out_specs=pl.BlockSpec((rows, 2 * width), lambda i, at: (at[0], 0)),
        ),
        out_shape=shape,
        input_output_aliases={} if out is None else {2: 0},
        compiler_params=params(),
        name="unpack_into",
    )(side, value, *([] if out is None else [out]))


def around(value, axis):
    size = lax.axis_size(axis)
    return [value] + [
        lax.ppermute(value, axis, [(i, (i + shift) % size) for i in range(size)]) for shift in range(1, size)
    ]


def in_order(core, mine, other):
    return [jnp.where(core == 0, mine, other), jnp.where(core == 0, other, mine)]


def local(slices, context_factor, mixing, year_weights):
    years_here = slices.shape[0]
    rank = mixing.shape[0]
    x_count, cores = lax.axis_size("x"), lax.axis_size("core")
    word_count, parts = lax.axis_size("word"), lax.axis_size("context")
    x_me, core, me = lax.axis_index("x"), lax.axis_index("core"), lax.axis_index("context")
    year_first = (x_me * cores + core) * years_here
    at = jnp.stack([me, core, year_first]).astype(jnp.int32)
    local_weights = lax.dynamic_slice_in_dim(year_weights, year_first, years_here, 0)
    coupled = (local_weights[:, :, None] * mixing.T[None, :, :]).astype(BF16)
    weighted = (mixing[None, :, :] * local_weights[:, None, :]).astype(BF16)

    me_at, core_at = at[:1], core.astype(jnp.int32)[None]

    def send(value, shift):
        return lax.ppermute(value, "context", [(i, (i + shift) % parts) for i in range(parts)])

    middle = parts // 2
    order = ((middle, 1, 1), (1, middle, 2))
    arrived = []
    for shifts in order:
        sent = reduced_parts(slices, context_factor, me_at, parts, shifts, BF16)
        arrived += [send(value, shifts[0] + shifts[1] * i) for i, value in enumerate(sent)]
    (own,) = reduced_parts(slices, context_factor, me_at, parts, (0, 1, 1), F32)
    inverse, mixing_gram, weight_gram = context_inverse(own, mixing, year_weights)
    own_rows, *shares = rows_and_gram(me_at, inverse, [own] + arrived, word_count)
    gram_part = sum_all([shares[0]] + [send(shares[shift], shift) for shift in range(1, parts)])
    rows = around(own_rows, "context")
    distance = 1
    while distance < word_count:
        partner = distance if 2 * distance < word_count else word_count - 1
        got = lax.ppermute(gram_part, "word", [(i, i ^ partner) for i in range(word_count)])
        distance *= 2
        gram_part = sum_all([gram_part, got], *(rows[1:] if distance == word_count else []))
    grams = around(gram_part, "context")

    keep, give, side_keep, side_give = frames_and_context(
        at, slices, grams, rows, coupled, weighted, year_weights, mixing
    )

    swap = [(i, cores - 1 - i) for i in range(cores)]
    count = x_count * word_count
    both = add_cores(keep, lax.ppermute(give, "core", swap)).reshape(count, -1, rank)
    factor_half = sum_all(around(factor_share(core_at, both, context_factor, cores), "context"))
    factor_other = lax.ppermute(factor_half, "core", swap)
    side_got = lax.ppermute(side_give, "core", swap)
    both_parts = lax.all_to_all(both, ("x", "word"), 0, 0, tiled=True)
    packed = pack_sum(both_parts, inverse, factor_other, side_got)
    first, second = factor_inverses(core_at, packed, mixing_gram, weight_gram, factor_half, factor_other)
    spread = jnp.broadcast_to(packed.astype(jnp.float16)[None], (count,) + packed.shape)
    mine = lax.all_to_all(spread, ("x", "word"), 0, 0, tiled=True)
    sides = around(sum_all([side_keep, side_got], packed), "x")
    solved = solve_sides(packed, first, second, sides)
    solved = in_order(core, solved, lax.ppermute(solved, "core", swap))
    edge = rank // 2
    new_mixing = jnp.concatenate([solved[0][:edge], solved[1][:edge]])
    new_years = jnp.concatenate([solved[0][edge:], solved[1][edge:]])
    other = lax.ppermute(mine, "core", swap)
    new_context = unpack_into(core_at, mine.astype(F32), None)
    new_context = unpack_into(1 - core_at, other.astype(F32), new_context)
    return (new_mixing, new_context, new_years)


def solution(mesh):
    year_count, word_count, context_count = mesh.devices.shape
    cores = 2
    fine = Mesh(
        mesh.devices.reshape(year_count // cores, cores, word_count, context_count),
        ("x", "core", "word", "context"),
    )
    in_specs = (P(("x", "core"), "word", "context"), P("context", None), P(), P())
    out_specs = (P(), P("context", None), P())
    return jax.shard_map(local, mesh=fine, in_specs=in_specs, out_specs=out_specs, check_vma=False)
```

```python
import functools

import jax
import jax.numpy as jnp
from jax import lax
from jax.experimental import pallas as pl
from jax.experimental.pallas import tpu as pltpu
from jax.sharding import Mesh, PartitionSpec as P

NS_STEPS = 8
F32, BF16 = jnp.float32, jnp.bfloat16
HIGHEST = lax.Precision.HIGHEST
VMEM_BYTES = 48 * 1024 * 1024
VMEM_SPEC = pl.BlockSpec(memory_space=pltpu.VMEM)
SMEM_SPEC = pl.BlockSpec(memory_space=pltpu.SMEM)
ANY_SPEC = pl.BlockSpec(memory_space=pl.ANY)


def dot(a, b, contract=((1,), (0,)), precision=None):
    return lax.dot_general(a, b, (contract, ((), ())), precision=precision, preferred_element_type=F32)


def exact(a, b, contract=((1,), (0,))):
    return dot(a, b, contract, HIGHEST)


def halves(a):
    high = a.astype(BF16)
    return high, (a - high.astype(F32)).astype(BF16)


def thirds(a):
    high, rest = halves(a)
    return high, rest, (a - high.astype(F32) - rest.astype(F32)).astype(BF16)


def close(a, b, contract=((1,), (0,))):
    return dot(a[0], b[0], contract) + (dot(a[0], b[1], contract) + dot(a[1], b[0], contract))


def close_each(left, b):
    split = [halves(a) for a in left]
    highs, lows = [a[0] for a in split], [a[1] for a in split]
    size = left[0].shape[0]
    by_high = dot(jnp.concatenate(highs + lows), b[0])
    by_low = dot(jnp.concatenate(highs), b[1])
    parts = [by_high[i * size : (i + 1) * size] for i in range(2 * len(left))]
    return [
        parts[i] + (by_low[i * size : (i + 1) * size] + parts[len(left) + i]) for i in range(len(left))
    ]


def params():
    return pltpu.CompilerParams(vmem_limit_bytes=VMEM_BYTES)


def reduced_kernel(count, me_ref, slices_ref, factor_ref, *out_refs):
    step, y = pl.program_id(0), pl.program_id(1)
    product = dot(slices_ref[0], factor_ref[...])
    for i in range(count):

        @pl.when(step == i)
        def _():
            out_refs[i][y] = product.astype(out_refs[i].dtype)


def reduced_parts(slices, context_factor, me, parts, shifts, dtype):
    first, stride, count = shifts
    years, rows, columns = slices.shape
    rank = context_factor.shape[1]
    chunk = rows // parts
    out_block = pl.BlockSpec((years, chunk, rank), lambda s, y, m: (0, 0, 0))
    return pl.pallas_call(
        functools.partial(reduced_kernel, count),
        grid_spec=pltpu.PrefetchScalarGridSpec(
            num_scalar_prefetch=1,
            grid=(count, years),
            in_specs=[
                pl.BlockSpec(
                    (1, chunk, columns), lambda s, y, m: (y, lax.rem(m[0] + first + s * stride, parts), 0)
                ),
                pl.BlockSpec((columns, rank), lambda s, y, m: (0, 0)),
            ],
            out_specs=[out_block] * count,
        ),
        out_shape=[jax.ShapeDtypeStruct((years, chunk, rank), dtype)] * count,
        compiler_params=params(),
        name="reduced_parts",
    )(me, slices, context_factor)


def factor_share_kernel(at_ref, after_ref, factor_ref, out_ref, scratch):
    share = out_ref.shape[0]
    scratch[...] = dot(factor_ref[...], factor_ref[...], ((0,), (0,)))
    out_ref[...] = scratch[pl.ds(pl.multiple_of(at_ref[0] * share, share), share), :]


def factor_share(me, after, context_factor, shares):
    rank = context_factor.shape[1]
    return pl.pallas_call(
        factor_share_kernel,
        in_specs=[SMEM_SPEC, ANY_SPEC, VMEM_SPEC],
        out_specs=VMEM_SPEC,
        out_shape=jax.ShapeDtypeStruct((rank // shares, rank), F32),
        scratch_shapes=[pltpu.VMEM((rank, rank), F32)],
        compiler_params=params(),
        name="factor_share",
    )(me, after, context_factor)


def rows_kernel(me_ref, after_ref, *refs):
    count = (len(refs) - 2) // 2
    parts, rows_ref, shares, gram_ref = refs[:count], refs[count], refs[count + 1 : -1], refs[-1]
    years, _, rank = rows_ref.shape
    half = rank // 2
    for y in range(years):
        total = parts[0][y]
        for part in parts[1:]:
            total += part[y].astype(F32)
        rows = total.astype(rows_ref.dtype)
        rows_ref[y] = rows
        gram = dot(rows, rows, ((0,), (0,)))
        first = 3 * half * y
        gram_ref[first : first + half, :] = gram[:half, :half]
        gram_ref[first + half : first + 2 * half, :] = gram[:half, half:]
        gram_ref[first + 2 * half : first + 3 * half, :] = gram[half:, half:]
    words, height, _ = shares[0].shape
    for shift, share in enumerate(shares):
        owner = lax.rem(me_ref[0] + shift, count)
        for w in range(words):
            at = pl.multiple_of((owner * words + w) * height, height)
            share[w] = gram_ref[pl.ds(at, height), :]


def rows_and_gram(me, after, parts, words):
    count = len(parts)
    years, _, rank = parts[0].shape
    gram_rows = 3 * years * rank // 2
    share = jax.ShapeDtypeStruct((words, gram_rows // (count * words), rank // 2), F32)
    return pl.pallas_call(
        rows_kernel,
        in_specs=[SMEM_SPEC, ANY_SPEC] + [VMEM_SPEC] * count,
        out_specs=[VMEM_SPEC] * (1 + count),
        out_shape=[jax.ShapeDtypeStruct(parts[0].shape, BF16)] + [share] * count,
        scratch_shapes=[pltpu.VMEM((gram_rows, rank // 2), F32)],
        compiler_params=params(),
        name="rows_and_gram",
    )(me, after, *parts)


NEWTON_ROUGH = 4
NEWTON_MOST = 48
NEWTON_SETTLED = 4e-8


def identity(size):
    rows = lax.broadcasted_iota(jnp.int32, (size, size), 0)
    return jnp.where(rows == lax.broadcasted_iota(jnp.int32, (size, size), 1), 1.0, 0.0)


def inverses(grams, scaled_ref, guess_ref):
    count, size = len(grams), grams[0].shape[0]
    eye = identity(size)
    scales = []
    for b, gram in enumerate(grams):
        diagonal = gram * eye
        across = lax.rsqrt(jnp.sum(diagonal, axis=0, keepdims=True))
        down = lax.rsqrt(jnp.sum(diagonal, axis=1, keepdims=True))
        scaled = gram * across * down
        bound = jnp.max(jnp.sum(jnp.abs(scaled), axis=0, keepdims=True), axis=1, keepdims=True)
        scaled_ref[b] = scaled
        guess_ref[b] = (2.0 * eye - scaled / bound) / bound
        scales.append((across, down))

    def rough(_, carry):
        for b in range(count):
            guess = guess_ref[b].astype(BF16)
            rest = eye - dot(scaled_ref[b].astype(BF16), guess)
            guess_ref[b] = guess_ref[b] + dot(guess, rest.astype(BF16))
        return carry

    def step(state):
        most = None
        for b in range(count):
            guess = guess_ref[b]
            rest = eye - exact(scaled_ref[b], guess)
            guess_ref[b] = guess + close(halves(guess), halves(rest))
            square = jnp.sum(rest * rest)
            most = square if most is None else jnp.maximum(most, square)
        return state[0] + 1, most

    lax.fori_loop(0, NEWTON_ROUGH, rough, 0)
    lax.while_loop(
        lambda state: (state[0] < NEWTON_MOST) & (state[1] > NEWTON_SETTLED), step, (0, jnp.float32(1.0))
    )
    return [guess_ref[b] * across * down for b, (across, down) in enumerate(scales)]


def newton_scratch(count, rank):
    return [pltpu.VMEM((count, rank, rank), F32)] * 2


def context_inverse_kernel(after_ref, mixing_ref, weights_ref, inverse_ref, first_ref, second_ref, *scratch):
    first_ref[...] = exact(mixing_ref[...], mixing_ref[...], ((0,), (0,)))
    second_ref[...] = exact(weights_ref[...], weights_ref[...], ((0,), (0,)))
    (inverse,) = inverses([first_ref[...] * second_ref[...]], *scratch)
    inverse_ref[...] = inverse


def context_inverse(after, mixing, year_weights):
    return pl.pallas_call(
        context_inverse_kernel,
        in_specs=[ANY_SPEC] + [VMEM_SPEC] * 2,
        out_specs=[VMEM_SPEC] * 3,
        out_shape=[jax.ShapeDtypeStruct(mixing.shape, F32)] * 3,
        scratch_shapes=newton_scratch(1, mixing.shape[0]),
        compiler_params=params(),
        name="context_inverse",
    )(after, mixing, year_weights)


def frames_kernel(parts, at_ref, slices_ref, *refs):
    grams, rows = refs[:parts], refs[parts : 2 * parts]
    coupled_ref, weighted_ref, weights_ref, mixing_ref = refs[2 * parts : 2 * parts + 4]
    keep_ref, give_ref, side_keep_ref, side_give_ref = refs[2 * parts + 4 : 2 * parts + 8]
    tile_ref, packed_ref, gram_ref, half_ref, polar_ref, rows_ref, lifted_ref, side_ref, sem = refs[2 * parts + 8 :]
    years, tile_rows, columns = tile_ref.shape
    rank = mixing_ref.shape[0]
    load = pltpu.make_async_copy(slices_ref, tile_ref, sem)
    load.start()
    me, core, year_first = at_ref[0], at_ref[1], at_ref[2]
    words, share, _ = grams[0].shape
    chunk = rows[0].shape[1]
    for shift in range(parts):
        owner = lax.rem(me + (parts - shift), parts)
        for w in range(words):
            at = pl.multiple_of((owner * words + w) * share, share)
            packed_ref[pl.ds(at, share), :] = grams[shift][w]
        for y in range(years):
            at = pl.multiple_of(owner * chunk, chunk)
            rows_ref[y, pl.ds(at, chunk), :] = rows[shift][y]
    edge = rank // 2
    for y in range(years):
        first = 3 * edge * y
        cross = packed_ref[first + edge : first + 2 * edge, :]
        gram_ref[y, :edge, :edge] = packed_ref[first : first + edge, :]
        gram_ref[y, :edge, edge:] = cross
        gram_ref[y, edge:, :edge] = cross.T
        gram_ref[y, edge:, edge:] = packed_ref[first + 2 * edge : first + 3 * edge, :]

    row_at = lax.broadcasted_iota(jnp.int32, (rank, rank), 0)
    diagonal = row_at == lax.broadcasted_iota(jnp.int32, (rank, rank), 1)
    coupled = [coupled_ref[y] for y in range(years)]
    half_way = [sum(dot(coupled[y], p, ((0,), (0,))) for p in thirds(gram_ref[y])) for y in range(years)]
    squares = [sum(dot(p, coupled[y]) for p in thirds(half_way[y])) for y in range(years)]
    traces = [
        jnp.sum(jnp.sum(jnp.where(diagonal, s, 0.0), axis=1, keepdims=True), axis=0, keepdims=True) + 1e-06
        for s in squares
    ]
    for y in range(years):
        gram_ref[y] = squares[y] / traces[y]
        half_ref[y] = half_way[y]
        polar_ref[y] = jnp.where(diagonal, 1.0, 0.0)

    def factor_of(y):
        return halves(jnp.where(diagonal, 1.5, 0.0) - 0.5 * gram_ref[y])

    def sweep(_, carry):
        factor = [factor_of(y) for y in range(years)]
        both = [close_each([gram_ref[y], polar_ref[y]], factor[y]) for y in range(years)]
        for y in range(years):
            polar_ref[y] = both[y][1]
        for y in range(years):
            gram_ref[y] = close_each([both[y][0]], factor[y])[0]
        return carry

    lax.fori_loop(0, NS_STEPS - 1, sweep, 0)
    polar = [close(halves(polar_ref[y]), factor_of(y)) for y in range(years)]
    scale = [lax.rsqrt(t) for t in traces]
    lift = [sum(dot(p, weighted_ref[y]) for p in halves(polar[y])) for y in range(years)]
    lift = [sum(dot(coupled[y], p) for p in halves(lift[y])) * scale[y] for y in range(years)]
    side_ref[rank:, :] = jnp.zeros((side_ref.shape[0] - rank, rank), F32)
    mixing_part = None
    for y in range(years):
        through = close(halves(polar[y]), halves(half_ref[y]), ((0,), (0,))) * scale[y]
        term = weights_ref[pl.ds(year_first + y, 1), :] * through
        mixing_part = term if mixing_part is None else mixing_part + term
        side_ref[pl.ds(rank + year_first + y, 1), :] = jnp.sum(
            mixing_ref[...] * through, axis=0, keepdims=True
        )
    side_ref[:rank, :] = mixing_part
    half_years = (side_ref.shape[0] - rank) // 2
    for target, side in ((side_keep_ref, core), (side_give_ref, 1 - core)):
        target[:edge, :] = side_ref[pl.ds(pl.multiple_of(side * edge, edge), edge), :]
        target[edge:, :] = side_ref[pl.ds(pl.multiple_of(rank + side * half_years, half_years), half_years), :]
    for y in range(years):
        high, low = halves(lift[y])
        lifted = dot(jnp.concatenate([high, low], axis=1), rows_ref[y], ((0,), (1,)))
        lifted = lifted[:rank] + lifted[rank:]
        lifted_ref[:, y * tile_rows : (y + 1) * tile_rows] = lifted.astype(BF16)
    load.wait()
    half = columns // 2
    width = rank
    for target, side in ((give_ref, 1 - core), (keep_ref, core)):

        @pl.loop(0, half // width)
        def _(block):
            at = pl.multiple_of(side * half + block * width, width)
            total = dot(lifted_ref[:, :tile_rows], tile_ref[0, :, pl.ds(at, width)])
            for y in range(1, years):
                total += dot(
                    lifted_ref[:, y * tile_rows : (y + 1) * tile_rows], tile_ref[y, :, pl.ds(at, width)]
                )
            out_at = pl.ds(pl.multiple_of(block * width, width), width)
            target[out_at, :] = total.T.astype(target.dtype)


def frames_and_context(at, slices, grams, rows, coupled, weighted, year_weights, mixing):
    parts = len(grams)
    years, tile_rows, columns = slices.shape
    rank = mixing.shape[0]
    side_rows = rank + year_weights.shape[0]
    return pl.pallas_call(
        functools.partial(frames_kernel, parts),
        in_specs=[SMEM_SPEC, ANY_SPEC] + [VMEM_SPEC] * (2 * parts + 4),
        out_specs=[VMEM_SPEC] * 4,
        out_shape=[
            jax.ShapeDtypeStruct((columns // 2, rank), F32),
            jax.ShapeDtypeStruct((columns // 2, rank), BF16),
            jax.ShapeDtypeStruct((side_rows // 2, rank), F32),
            jax.ShapeDtypeStruct((side_rows // 2, rank), F32),
        ],
        scratch_shapes=[
            pltpu.VMEM((years, tile_rows, columns), BF16),
            pltpu.VMEM((3 * years * rank // 2, rank // 2), F32),
            pltpu.VMEM((years, rank, rank), F32),
            pltpu.VMEM((years, rank, rank), F32),
            pltpu.VMEM((years, rank, rank), F32),
            pltpu.VMEM((years, tile_rows, rank), BF16),
            pltpu.VMEM((rank, years * tile_rows), BF16),
            pltpu.VMEM((side_rows, rank), F32),
            pltpu.SemaphoreType.DMA(()),
        ],
        compiler_params=params(),
        cost_estimate=pl.CostEstimate(
            flops=12_000_000_000, bytes_accessed=40_000_000, transcendentals=0
        ),
        name="frames_and_context",
    )(at, slices, *grams, *rows, coupled, weighted, year_weights, mixing)


SCALE_ROWS = 8


def pack_kernel(parts_ref, inverse_ref, *refs):
    packed_ref = refs[-1]
    count, height, rank = parts_ref.shape
    total = parts_ref[0].astype(F32)
    for i in range(1, count):
        total += parts_ref[i].astype(F32)
    total = exact(total, inverse_ref[...])
    most = jnp.max(jnp.max(jnp.abs(total), axis=1, keepdims=True), axis=0, keepdims=True)
    power = jnp.clip(jnp.ceil(jnp.log2(most)), -120.0, 120.0)
    total = total * jnp.exp2(-power)
    packed_ref[:height, :] = total[:, : rank // 2]
    packed_ref[height : 2 * height, :] = total[:, rank // 2 :]
    packed_ref[2 * height :, :] = jnp.broadcast_to(power, (SCALE_ROWS, rank // 2))


def pack_sum(parts, inverse, *after):
    _, height, rank = parts.shape
    return pl.pallas_call(
        pack_kernel,
        in_specs=[VMEM_SPEC] * 2 + [ANY_SPEC] * len(after),
        out_specs=VMEM_SPEC,
        out_shape=jax.ShapeDtypeStruct((2 * height + SCALE_ROWS, rank // 2), F32),
        compiler_params=params(),
        name="pack_sum",
    )(parts, inverse, *after)


def sum_kernel(count, *refs):
    total = refs[0][...]
    for ref in refs[1:count]:
        total += ref[...]
    refs[-1][...] = total


def sum_all(values, *after):
    return pl.pallas_call(
        functools.partial(sum_kernel, len(values)),
        in_specs=[VMEM_SPEC] * len(values) + [ANY_SPEC] * len(after),
        out_specs=VMEM_SPEC,
        out_shape=jax.ShapeDtypeStruct(values[0].shape, values[0].dtype),
        compiler_params=params(),
        name="sum_all",
    )(*values, *after)


def add_cores_kernel(keep_ref, got_ref, out_ref):
    out_ref[...] = (keep_ref[...] + got_ref[...].astype(F32)).astype(out_ref.dtype)


def add_cores(keep, got):
    return pl.pallas_call(
        add_cores_kernel,
        in_specs=[VMEM_SPEC] * 2,
        out_specs=VMEM_SPEC,
        out_shape=jax.ShapeDtypeStruct(keep.shape, BF16),
        compiler_params=params(),
        name="add_cores",
    )(keep, got)


def factor_inverses_kernel(core_ref, after_ref, mixing_ref, weights_ref, mine_ref, other_ref, *refs):
    first_ref, second_ref, gram_ref = refs[:3]
    edge = mine_ref.shape[0]
    for piece, side in ((mine_ref, core_ref[0]), (other_ref, 1 - core_ref[0])):
        gram_ref[pl.ds(pl.multiple_of(side * edge, edge), edge), :] = piece[...]
    factor_gram = gram_ref[...]
    first, second = inverses([factor_gram * weights_ref[...], mixing_ref[...] * factor_gram], *refs[3:])
    first_ref[...] = first
    second_ref[...] = second


def factor_inverses(core, after, mixing_gram, weight_gram, mine, other):
    rank = mixing_gram.shape[0]
    return pl.pallas_call(
        factor_inverses_kernel,
        in_specs=[SMEM_SPEC, ANY_SPEC] + [VMEM_SPEC] * 4,
        out_specs=[VMEM_SPEC] * 2,
        out_shape=[jax.ShapeDtypeStruct((rank, rank), F32)] * 2,
        scratch_shapes=[pltpu.VMEM((rank, rank), F32)] + newton_scratch(2, rank),
        compiler_params=params(),
        name="factor_inverses",
    )(core, after, mixing_gram, weight_gram, mine, other)


def solve_kernel(core_ref, after_ref, first_ref, second_ref, mine_ref, other_ref, *refs):
    mixing_ref, years_ref, mixing_side, years_side = refs
    edge = first_ref.shape[0] // 2
    height = mine_ref.shape[0] - edge
    for piece, side in ((mine_ref, core_ref[0]), (other_ref, 1 - core_ref[0])):
        mixing_side[pl.ds(pl.multiple_of(side * edge, edge), edge), :] = piece[:edge, :]
        years_side[pl.ds(pl.multiple_of(side * height, height), height), :] = piece[edge:, :]
    mixing_ref[...] = exact(mixing_side[...], first_ref[...])
    years_ref[...] = exact(years_side[...], second_ref[...])


def solve_sides(core, after, first_inverse, second_inverse, mine, other):
    rank = first_inverse.shape[0]
    years = 2 * (mine.shape[0] - rank // 2)
    return pl.pallas_call(
        solve_kernel,
        in_specs=[SMEM_SPEC, ANY_SPEC] + [VMEM_SPEC] * 4,
        out_specs=[VMEM_SPEC] * 2,
        out_shape=[
            jax.ShapeDtypeStruct((rank, rank), F32),
            jax.ShapeDtypeStruct((years, rank), F32),
        ],
        scratch_shapes=[pltpu.VMEM((rank, rank), F32), pltpu.VMEM((years, rank), F32)],
        compiler_params=params(),
        name="solve_sides",
    )(core, after, first_inverse, second_inverse, mine, other)


def unpack_kernel(side_ref, value_ref, *refs):
    out_ref = refs[-1]
    count, height, width = value_ref.shape
    height = (height - SCALE_ROWS) // 2
    for i in range(count):
        value = value_ref[i]
        scale = jnp.exp2(value[2 * height : 2 * height + 1, :])
        at = pl.ds(i * height, height)
        out_ref[at, :width] = value[:height] * scale
        out_ref[at, width:] = value[height : 2 * height] * scale


def unpack_into(side, value, out):
    count, height, width = value.shape
    rows = count * ((height - SCALE_ROWS) // 2)
    shape = jax.ShapeDtypeStruct((2 * rows, 2 * width), F32)
    whole = pl.BlockSpec(value.shape, lambda i, at: (0, 0, 0))
    return pl.pallas_call(
        unpack_kernel,
        grid_spec=pltpu.PrefetchScalarGridSpec(
            num_scalar_prefetch=1,
            grid=(1,),
            in_specs=[whole] + ([] if out is None else [ANY_SPEC]),
            out_specs=pl.BlockSpec((rows, 2 * width), lambda i, at: (at[0], 0)),
        ),
        out_shape=shape,
        input_output_aliases={} if out is None else {2: 0},
        compiler_params=params(),
        name="unpack_into",
    )(side, value, *([] if out is None else [out]))


def around(value, axis):
    size = lax.axis_size(axis)
    return [value] + [
        lax.ppermute(value, axis, [(i, (i + shift) % size) for i in range(size)]) for shift in range(1, size)
    ]


def local(slices, context_factor, mixing, year_weights):
    years_here = slices.shape[0]
    rank = mixing.shape[0]
    x_count, cores = lax.axis_size("x"), lax.axis_size("core")
    word_count, parts = lax.axis_size("word"), lax.axis_size("context")
    x_me, core, me = lax.axis_index("x"), lax.axis_index("core"), lax.axis_index("context")
    year_first = (x_me * cores + core) * years_here
    at = jnp.stack([me, core, year_first]).astype(jnp.int32)
    local_weights = lax.dynamic_slice_in_dim(year_weights, year_first, years_here, 0)
    coupled = (local_weights[:, :, None] * mixing.T[None, :, :]).astype(BF16)
    weighted = (mixing[None, :, :] * local_weights[:, None, :]).astype(BF16)

    me_at, core_at = at[:1], core.astype(jnp.int32)[None]

    def send(value, shift):
        return lax.ppermute(value, "context", [(i, (i + shift) % parts) for i in range(parts)])

    middle = parts // 2
    order = ((middle, 1, 1), (1, middle, 2))
    arrived = []
    for shifts in order:
        sent = reduced_parts(slices, context_factor, me_at, parts, shifts, BF16)
        arrived += [send(value, shifts[0] + shifts[1] * i) for i, value in enumerate(sent)]
    (own,) = reduced_parts(slices, context_factor, me_at, parts, (0, 1, 1), F32)
    inverse, mixing_gram, weight_gram = context_inverse(own, mixing, year_weights)
    own_rows, *shares = rows_and_gram(me_at, inverse, [own] + arrived, word_count)
    gram_part = sum_all([shares[0]] + [send(shares[shift], shift) for shift in range(1, parts)])
    rows = around(own_rows, "context")
    distance = 1
    while distance < word_count:
        partner = distance if 2 * distance < word_count else word_count - 1
        got = lax.ppermute(gram_part, "word", [(i, i ^ partner) for i in range(word_count)])
        distance *= 2
        gram_part = sum_all([gram_part, got], *(rows[1:] if distance == word_count else []))
    grams = around(gram_part, "context")

    keep, give, side_keep, side_give = frames_and_context(
        at, slices, grams, rows, coupled, weighted, year_weights, mixing
    )

    swap = [(i, cores - 1 - i) for i in range(cores)]
    count = x_count * word_count
    both = add_cores(keep, lax.ppermute(give, "core", swap)).reshape(count, -1, rank)
    factor_half = sum_all(around(factor_share(core_at, both, context_factor, cores), "context"))
    factor_other = lax.ppermute(factor_half, "core", swap)
    side_got = lax.ppermute(side_give, "core", swap)
    both_parts = lax.all_to_all(both, ("x", "word"), 0, 0, tiled=True)
    packed = pack_sum(both_parts, inverse, factor_other, side_got)
    first, second = factor_inverses(core_at, packed, mixing_gram, weight_gram, factor_half, factor_other)
    spread = jnp.broadcast_to(packed.astype(jnp.float16)[None], (count,) + packed.shape)
    mine = lax.all_to_all(spread, ("x", "word"), 0, 0, tiled=True)
    side_half = sum_all(around(sum_all([side_keep, side_got], packed), "x"), first)
    side_other = lax.ppermute(side_half, "core", swap)
    new_mixing, new_years = solve_sides(core_at, packed, first, second, side_half, side_other)
    mine, new_mixing = lax.optimization_barrier((mine, new_mixing))
    other = lax.ppermute(mine, "core", swap)
    new_context = unpack_into(core_at, mine.astype(F32), None)
    new_context = unpack_into(1 - core_at, other.astype(F32), new_context)
    return (new_mixing, new_context, new_years)


def solution(mesh):
    year_count, word_count, context_count = mesh.devices.shape
    cores = 2
    fine = Mesh(
        mesh.devices.reshape(year_count // cores, cores, word_count, context_count),
        ("x", "core", "word", "context"),
    )
    in_specs = (P(("x", "core"), "word", "context"), P("context", None), P(), P())
    out_specs = (P(), P("context", None), P())
    return jax.shard_map(local, mesh=fine, in_specs=in_specs, out_specs=out_specs, check_vma=False)
```

```python
import functools

import jax
import jax.numpy as jnp
from jax import lax
from jax.experimental import pallas as pl
from jax.experimental.pallas import tpu as pltpu
from jax.sharding import Mesh, PartitionSpec as P

NS_STEPS = 8
F32, BF16 = jnp.float32, jnp.bfloat16
HIGHEST = lax.Precision.HIGHEST
VMEM_BYTES = 48 * 1024 * 1024
VMEM_SPEC = pl.BlockSpec(memory_space=pltpu.VMEM)
SMEM_SPEC = pl.BlockSpec(memory_space=pltpu.SMEM)
ANY_SPEC = pl.BlockSpec(memory_space=pl.ANY)


def dot(a, b, contract=((1,), (0,)), precision=None):
    return lax.dot_general(a, b, (contract, ((), ())), precision=precision, preferred_element_type=F32)


def exact(a, b, contract=((1,), (0,))):
    return dot(a, b, contract, HIGHEST)


def halves(a):
    high = a.astype(BF16)
    return high, (a - high.astype(F32)).astype(BF16)


def thirds(a):
    high, rest = halves(a)
    return high, rest, (a - high.astype(F32) - rest.astype(F32)).astype(BF16)


def close(a, b, contract=((1,), (0,))):
    return dot(a[0], b[0], contract) + (dot(a[0], b[1], contract) + dot(a[1], b[0], contract))


def close_each(left, b):
    split = [halves(a) for a in left]
    highs, lows = [a[0] for a in split], [a[1] for a in split]
    size = left[0].shape[0]
    by_high = dot(jnp.concatenate(highs + lows), b[0])
    by_low = dot(jnp.concatenate(highs), b[1])
    parts = [by_high[i * size : (i + 1) * size] for i in range(2 * len(left))]
    return [
        parts[i] + (by_low[i * size : (i + 1) * size] + parts[len(left) + i]) for i in range(len(left))
    ]


def params():
    return pltpu.CompilerParams(vmem_limit_bytes=VMEM_BYTES)


def reduced_kernel(count, me_ref, slices_ref, factor_ref, *out_refs):
    step, y = pl.program_id(0), pl.program_id(1)
    product = dot(slices_ref[0], factor_ref[...])
    for i in range(count):

        @pl.when(step == i)
        def _():
            out_refs[i][y] = product.astype(out_refs[i].dtype)


def reduced_parts(slices, context_factor, me, parts, shifts, dtype):
    first, stride, count = shifts
    years, rows, columns = slices.shape
    rank = context_factor.shape[1]
    chunk = rows // parts
    out_block = pl.BlockSpec((years, chunk, rank), lambda s, y, m: (0, 0, 0))
    return pl.pallas_call(
        functools.partial(reduced_kernel, count),
        grid_spec=pltpu.PrefetchScalarGridSpec(
            num_scalar_prefetch=1,
            grid=(count, years),
            in_specs=[
                pl.BlockSpec(
                    (1, chunk, columns), lambda s, y, m: (y, lax.rem(m[0] + first + s * stride, parts), 0)
                ),
                pl.BlockSpec((columns, rank), lambda s, y, m: (0, 0)),
            ],
            out_specs=[out_block] * count,
        ),
        out_shape=[jax.ShapeDtypeStruct((years, chunk, rank), dtype)] * count,
        compiler_params=params(),
        name="reduced_parts",
    )(me, slices, context_factor)


def factor_share_kernel(at_ref, after_ref, factor_ref, out_ref, scratch):
    share = out_ref.shape[0]
    scratch[...] = dot(factor_ref[...], factor_ref[...], ((0,), (0,)))
    out_ref[...] = scratch[pl.ds(pl.multiple_of(at_ref[0] * share, share), share), :]


def factor_share(me, after, context_factor, shares):
    rank = context_factor.shape[1]
    return pl.pallas_call(
        factor_share_kernel,
        in_specs=[SMEM_SPEC, ANY_SPEC, VMEM_SPEC],
        out_specs=VMEM_SPEC,
        out_shape=jax.ShapeDtypeStruct((rank // shares, rank), F32),
        scratch_shapes=[pltpu.VMEM((rank, rank), F32)],
        compiler_params=params(),
        name="factor_share",
    )(me, after, context_factor)


def rows_kernel(me_ref, after_ref, *refs):
    count = (len(refs) - 2) // 2
    parts, rows_ref, shares, gram_ref = refs[:count], refs[count], refs[count + 1 : -1], refs[-1]
    years, _, rank = rows_ref.shape
    half = rank // 2
    for y in range(years):
        total = parts[0][y]
        for part in parts[1:]:
            total += part[y].astype(F32)
        rows = total.astype(rows_ref.dtype)
        rows_ref[y] = rows
        gram = dot(rows, rows, ((0,), (0,)))
        first = 3 * half * y
        gram_ref[first : first + half, :] = gram[:half, :half]
        gram_ref[first + half : first + 2 * half, :] = gram[:half, half:]
        gram_ref[first + 2 * half : first + 3 * half, :] = gram[half:, half:]
    words, height, _ = shares[0].shape
    for shift, share in enumerate(shares):
        owner = lax.rem(me_ref[0] + shift, count)
        for w in range(words):
            at = pl.multiple_of((owner * words + w) * height, height)
            share[w] = gram_ref[pl.ds(at, height), :]


def rows_and_gram(me, after, parts, words):
    count = len(parts)
    years, _, rank = parts[0].shape
    gram_rows = 3 * years * rank // 2
    share = jax.ShapeDtypeStruct((words, gram_rows // (count * words), rank // 2), F32)
    return pl.pallas_call(
        rows_kernel,
        in_specs=[SMEM_SPEC, ANY_SPEC] + [VMEM_SPEC] * count,
        out_specs=[VMEM_SPEC] * (1 + count),
        out_shape=[jax.ShapeDtypeStruct(parts[0].shape, BF16)] + [share] * count,
        scratch_shapes=[pltpu.VMEM((gram_rows, rank // 2), F32)],
        compiler_params=params(),
        name="rows_and_gram",
    )(me, after, *parts)


NEWTON_ROUGH = 4
NEWTON_MOST = 48
NEWTON_SETTLED = 4e-8


def identity(size):
    rows = lax.broadcasted_iota(jnp.int32, (size, size), 0)
    return jnp.where(rows == lax.broadcasted_iota(jnp.int32, (size, size), 1), 1.0, 0.0)


def inverses(grams, scaled_ref, guess_ref):
    count, size = len(grams), grams[0].shape[0]
    eye = identity(size)
    scales = []
    for b, gram in enumerate(grams):
        diagonal = gram * eye
        across = lax.rsqrt(jnp.sum(diagonal, axis=0, keepdims=True))
        down = lax.rsqrt(jnp.sum(diagonal, axis=1, keepdims=True))
        scaled = gram * across * down
        bound = jnp.max(jnp.sum(jnp.abs(scaled), axis=0, keepdims=True), axis=1, keepdims=True)
        scaled_ref[b] = scaled
        guess_ref[b] = (2.0 * eye - scaled / bound) / bound
        scales.append((across, down))

    def rough(_, carry):
        for b in range(count):
            guess = guess_ref[b].astype(BF16)
            rest = eye - dot(scaled_ref[b].astype(BF16), guess)
            guess_ref[b] = guess_ref[b] + dot(guess, rest.astype(BF16))
        return carry

    def step(state):
        most = None
        for b in range(count):
            guess = guess_ref[b]
            rest = eye - exact(scaled_ref[b], guess)
            guess_ref[b] = guess + close(halves(guess), halves(rest))
            square = jnp.sum(rest * rest)
            most = square if most is None else jnp.maximum(most, square)
        return state[0] + 1, most

    lax.fori_loop(0, NEWTON_ROUGH, rough, 0)
    lax.while_loop(
        lambda state: (state[0] < NEWTON_MOST) & (state[1] > NEWTON_SETTLED), step, (0, jnp.float32(1.0))
    )
    return [guess_ref[b] * across * down for b, (across, down) in enumerate(scales)]


def newton_scratch(count, rank):
    return [pltpu.VMEM((count, rank, rank), F32)] * 2


def context_inverse_kernel(after_ref, mixing_ref, weights_ref, inverse_ref, first_ref, second_ref, *scratch):
    first_ref[...] = exact(mixing_ref[...], mixing_ref[...], ((0,), (0,)))
    second_ref[...] = exact(weights_ref[...], weights_ref[...], ((0,), (0,)))
    (inverse,) = inverses([first_ref[...] * second_ref[...]], *scratch)
    inverse_ref[...] = inverse


def context_inverse(after, mixing, year_weights):
    return pl.pallas_call(
        context_inverse_kernel,
        in_specs=[ANY_SPEC] + [VMEM_SPEC] * 2,
        out_specs=[VMEM_SPEC] * 3,
        out_shape=[jax.ShapeDtypeStruct(mixing.shape, F32)] * 3,
        scratch_shapes=newton_scratch(1, mixing.shape[0]),
        compiler_params=params(),
        name="context_inverse",
    )(after, mixing, year_weights)


def frames_kernel(parts, at_ref, slices_ref, *refs):
    grams, rows = refs[:parts], refs[parts : 2 * parts]
    coupled_ref, weighted_ref, weights_ref, mixing_ref = refs[2 * parts : 2 * parts + 4]
    keep_ref, give_ref, side_keep_ref, side_give_ref = refs[2 * parts + 4 : 2 * parts + 8]
    tile_ref, packed_ref, gram_ref, half_ref, polar_ref, rows_ref, lifted_ref, side_ref, sem = refs[2 * parts + 8 :]
    years, tile_rows, columns = tile_ref.shape
    rank = mixing_ref.shape[0]
    load = pltpu.make_async_copy(slices_ref, tile_ref, sem)
    load.start()
    me, core, year_first = at_ref[0], at_ref[1], at_ref[2]
    words, share, _ = grams[0].shape
    chunk = rows[0].shape[1]
    for shift in range(parts):
        owner = lax.rem(me + (parts - shift), parts)
        for w in range(words):
            at = pl.multiple_of((owner * words + w) * share, share)
            packed_ref[pl.ds(at, share), :] = grams[shift][w]
        for y in range(years):
            at = pl.multiple_of(owner * chunk, chunk)
            rows_ref[y, pl.ds(at, chunk), :] = rows[shift][y]
    edge = rank // 2
    for y in range(years):
        first = 3 * edge * y
        cross = packed_ref[first + edge : first + 2 * edge, :]
        gram_ref[y, :edge, :edge] = packed_ref[first : first + edge, :]
        gram_ref[y, :edge, edge:] = cross
        gram_ref[y, edge:, :edge] = cross.T
        gram_ref[y, edge:, edge:] = packed_ref[first + 2 * edge : first + 3 * edge, :]

    row_at = lax.broadcasted_iota(jnp.int32, (rank, rank), 0)
    diagonal = row_at == lax.broadcasted_iota(jnp.int32, (rank, rank), 1)
    coupled = [coupled_ref[y] for y in range(years)]
    half_way = [sum(dot(coupled[y], p, ((0,), (0,))) for p in thirds(gram_ref[y])) for y in range(years)]
    squares = [sum(dot(p, coupled[y]) for p in thirds(half_way[y])) for y in range(years)]
    traces = [
        jnp.sum(jnp.sum(jnp.where(diagonal, s, 0.0), axis=1, keepdims=True), axis=0, keepdims=True) + 1e-06
        for s in squares
    ]
    for y in range(years):
        gram_ref[y] = squares[y] / traces[y]
        half_ref[y] = half_way[y]
        polar_ref[y] = jnp.where(diagonal, 1.0, 0.0)

    def factor_of(y):
        return halves(jnp.where(diagonal, 1.5, 0.0) - 0.5 * gram_ref[y])

    def sweep(_, carry):
        factor = [factor_of(y) for y in range(years)]
        both = [close_each([gram_ref[y], polar_ref[y]], factor[y]) for y in range(years)]
        for y in range(years):
            polar_ref[y] = both[y][1]
        for y in range(years):
            gram_ref[y] = close_each([both[y][0]], factor[y])[0]
        return carry

    lax.fori_loop(0, NS_STEPS - 1, sweep, 0)
    polar = [close(halves(polar_ref[y]), factor_of(y)) for y in range(years)]
    scale = [lax.rsqrt(t) for t in traces]
    lift = [sum(dot(p, weighted_ref[y]) for p in halves(polar[y])) for y in range(years)]
    lift = [sum(dot(coupled[y], p) for p in halves(lift[y])) * scale[y] for y in range(years)]
    side_ref[rank:, :] = jnp.zeros((side_ref.shape[0] - rank, rank), F32)
    mixing_part = None
    for y in range(years):
        through = close(halves(polar[y]), halves(half_ref[y]), ((0,), (0,))) * scale[y]
        term = weights_ref[pl.ds(year_first + y, 1), :] * through
        mixing_part = term if mixing_part is None else mixing_part + term
        side_ref[pl.ds(rank + year_first + y, 1), :] = jnp.sum(
            mixing_ref[...] * through, axis=0, keepdims=True
        )
    side_ref[:rank, :] = mixing_part
    half_years = (side_ref.shape[0] - rank) // 2
    for target, side in ((side_keep_ref, core), (side_give_ref, 1 - core)):
        target[:edge, :] = side_ref[pl.ds(pl.multiple_of(side * edge, edge), edge), :]
        target[edge:, :] = side_ref[pl.ds(pl.multiple_of(rank + side * half_years, half_years), half_years), :]
    for y in range(years):
        high, low = halves(lift[y])
        lifted = dot(jnp.concatenate([high, low], axis=1), rows_ref[y], ((0,), (1,)))
        lifted = lifted[:rank] + lifted[rank:]
        lifted_ref[:, y * tile_rows : (y + 1) * tile_rows] = lifted.astype(BF16)
    load.wait()
    half = columns // 2
    width = rank
    for target, side in ((give_ref, 1 - core), (keep_ref, core)):

        @pl.loop(0, half // width)
        def _(block):
            at = pl.multiple_of(side * half + block * width, width)
            total = dot(lifted_ref[:, :tile_rows], tile_ref[0, :, pl.ds(at, width)])
            for y in range(1, years):
                total += dot(
                    lifted_ref[:, y * tile_rows : (y + 1) * tile_rows], tile_ref[y, :, pl.ds(at, width)]
                )
            out_at = pl.ds(pl.multiple_of(block * width, width), width)
            target[out_at, :] = total.T.astype(target.dtype)


def frames_and_context(at, slices, grams, rows, coupled, weighted, year_weights, mixing):
    parts = len(grams)
    years, tile_rows, columns = slices.shape
    rank = mixing.shape[0]
    side_rows = rank + year_weights.shape[0]
    return pl.pallas_call(
        functools.partial(frames_kernel, parts),
        in_specs=[SMEM_SPEC, ANY_SPEC] + [VMEM_SPEC] * (2 * parts + 4),
        out_specs=[VMEM_SPEC] * 4,
        out_shape=[
            jax.ShapeDtypeStruct((columns // 2, rank), F32),
            jax.ShapeDtypeStruct((columns // 2, rank), BF16),
            jax.ShapeDtypeStruct((side_rows // 2, rank), F32),
            jax.ShapeDtypeStruct((side_rows // 2, rank), F32),
        ],
        scratch_shapes=[
            pltpu.VMEM((years, tile_rows, columns), BF16),
            pltpu.VMEM((3 * years * rank // 2, rank // 2), F32),
            pltpu.VMEM((years, rank, rank), F32),
            pltpu.VMEM((years, rank, rank), F32),
            pltpu.VMEM((years, rank, rank), F32),
            pltpu.VMEM((years, tile_rows, rank), BF16),
            pltpu.VMEM((rank, years * tile_rows), BF16),
            pltpu.VMEM((side_rows, rank), F32),
            pltpu.SemaphoreType.DMA(()),
        ],
        compiler_params=params(),
        cost_estimate=pl.CostEstimate(
            flops=12_000_000_000, bytes_accessed=40_000_000, transcendentals=0
        ),
        name="frames_and_context",
    )(at, slices, *grams, *rows, coupled, weighted, year_weights, mixing)


SCALE_ROWS = 8


def pack_kernel(parts_ref, inverse_ref, *refs):
    packed_ref = refs[-1]
    count, height, rank = parts_ref.shape
    total = parts_ref[0].astype(F32)
    for i in range(1, count):
        total += parts_ref[i].astype(F32)
    total = exact(total, inverse_ref[...])
    most = jnp.max(jnp.max(jnp.abs(total), axis=1, keepdims=True), axis=0, keepdims=True)
    power = jnp.clip(jnp.ceil(jnp.log2(most)), -120.0, 120.0)
    total = total * jnp.exp2(-power)
    packed_ref[:height, :] = total[:, : rank // 2]
    packed_ref[height : 2 * height, :] = total[:, rank // 2 :]
    packed_ref[2 * height :, :] = jnp.broadcast_to(power, (SCALE_ROWS, rank // 2))


def pack_sum(parts, inverse, *after):
    _, height, rank = parts.shape
    return pl.pallas_call(
        pack_kernel,
        in_specs=[VMEM_SPEC] * 2 + [ANY_SPEC] * len(after),
        out_specs=VMEM_SPEC,
        out_shape=jax.ShapeDtypeStruct((2 * height + SCALE_ROWS, rank // 2), F32),
        compiler_params=params(),
        name="pack_sum",
    )(parts, inverse, *after)


def sum_kernel(count, *refs):
    total = refs[0][...]
    for ref in refs[1:count]:
        total += ref[...]
    refs[-1][...] = total


def sum_all(values, *after):
    return pl.pallas_call(
        functools.partial(sum_kernel, len(values)),
        in_specs=[VMEM_SPEC] * len(values) + [ANY_SPEC] * len(after),
        out_specs=VMEM_SPEC,
        out_shape=jax.ShapeDtypeStruct(values[0].shape, values[0].dtype),
        compiler_params=params(),
        name="sum_all",
    )(*values, *after)


def add_cores_kernel(keep_ref, got_ref, out_ref):
    out_ref[...] = (keep_ref[...] + got_ref[...].astype(F32)).astype(out_ref.dtype)


def add_cores(keep, got):
    return pl.pallas_call(
        add_cores_kernel,
        in_specs=[VMEM_SPEC] * 2,
        out_specs=VMEM_SPEC,
        out_shape=jax.ShapeDtypeStruct(keep.shape, BF16),
        compiler_params=params(),
        name="add_cores",
    )(keep, got)


def factor_inverses_kernel(core_ref, after_ref, mixing_ref, weights_ref, mine_ref, other_ref, *refs):
    first_ref, second_ref, gram_ref = refs[:3]
    edge = mine_ref.shape[0]
    for piece, side in ((mine_ref, core_ref[0]), (other_ref, 1 - core_ref[0])):
        gram_ref[pl.ds(pl.multiple_of(side * edge, edge), edge), :] = piece[...]
    factor_gram = gram_ref[...]
    first, second = inverses([factor_gram * weights_ref[...], mixing_ref[...] * factor_gram], *refs[3:])
    first_ref[...] = first
    second_ref[...] = second


def factor_inverses(core, after, mixing_gram, weight_gram, mine, other):
    rank = mixing_gram.shape[0]
    return pl.pallas_call(
        factor_inverses_kernel,
        in_specs=[SMEM_SPEC, ANY_SPEC] + [VMEM_SPEC] * 4,
        out_specs=[VMEM_SPEC] * 2,
        out_shape=[jax.ShapeDtypeStruct((rank, rank), F32)] * 2,
        scratch_shapes=[pltpu.VMEM((rank, rank), F32)] + newton_scratch(2, rank),
        compiler_params=params(),
        name="factor_inverses",
    )(core, after, mixing_gram, weight_gram, mine, other)


def solve_kernel(core_ref, after_ref, first_ref, second_ref, mine_ref, other_ref, *refs):
    mixing_ref, years_ref, mixing_side, years_side = refs
    edge = first_ref.shape[0] // 2
    height = mine_ref.shape[0] - edge
    for piece, side in ((mine_ref, core_ref[0]), (other_ref, 1 - core_ref[0])):
        mixing_side[pl.ds(pl.multiple_of(side * edge, edge), edge), :] = piece[:edge, :]
        years_side[pl.ds(pl.multiple_of(side * height, height), height), :] = piece[edge:, :]
    mixing_ref[...] = exact(mixing_side[...], first_ref[...])
    years_ref[...] = exact(years_side[...], second_ref[...])


def solve_sides(core, after, first_inverse, second_inverse, mine, other):
    rank = first_inverse.shape[0]
    years = 2 * (mine.shape[0] - rank // 2)
    return pl.pallas_call(
        solve_kernel,
        in_specs=[SMEM_SPEC, ANY_SPEC] + [VMEM_SPEC] * 4,
        out_specs=[VMEM_SPEC] * 2,
        out_shape=[
            jax.ShapeDtypeStruct((rank, rank), F32),
            jax.ShapeDtypeStruct((years, rank), F32),
        ],
        scratch_shapes=[pltpu.VMEM((rank, rank), F32), pltpu.VMEM((years, rank), F32)],
        compiler_params=params(),
        name="solve_sides",
    )(core, after, first_inverse, second_inverse, mine, other)


def unpack_kernel(side_ref, value_ref, *refs):
    out_ref = refs[-1]
    count, height, width = value_ref.shape
    height = (height - SCALE_ROWS) // 2
    for i in range(count):
        value = value_ref[i]
        scale = jnp.exp2(value[2 * height : 2 * height + 1, :])
        at = pl.ds(i * height, height)
        out_ref[at, :width] = value[:height] * scale
        out_ref[at, width:] = value[height : 2 * height] * scale


def unpack_into(side, value, out):
    count, height, width = value.shape
    rows = count * ((height - SCALE_ROWS) // 2)
    shape = jax.ShapeDtypeStruct((2 * rows, 2 * width), F32)
    whole = pl.BlockSpec(value.shape, lambda i, at: (0, 0, 0))
    return pl.pallas_call(
        unpack_kernel,
        grid_spec=pltpu.PrefetchScalarGridSpec(
            num_scalar_prefetch=1,
            grid=(1,),
            in_specs=[whole] + ([] if out is None else [ANY_SPEC]),
            out_specs=pl.BlockSpec((rows, 2 * width), lambda i, at: (at[0], 0)),
        ),
        out_shape=shape,
        input_output_aliases={} if out is None else {2: 0},
        compiler_params=params(),
        name="unpack_into",
    )(side, value, *([] if out is None else [out]))


def around(value, axis):
    size = lax.axis_size(axis)
    return [value] + [
        lax.ppermute(value, axis, [(i, (i + shift) % size) for i in range(size)]) for shift in range(1, size)
    ]


def local(slices, context_factor, mixing, year_weights):
    years_here = slices.shape[0]
    rank = mixing.shape[0]
    x_count, cores = lax.axis_size("x"), lax.axis_size("core")
    word_count, parts = lax.axis_size("word"), lax.axis_size("context")
    x_me, core, me = lax.axis_index("x"), lax.axis_index("core"), lax.axis_index("context")
    year_first = (x_me * cores + core) * years_here
    at = jnp.stack([me, core, year_first]).astype(jnp.int32)
    local_weights = lax.dynamic_slice_in_dim(year_weights, year_first, years_here, 0)
    coupled = (local_weights[:, :, None] * mixing.T[None, :, :]).astype(BF16)
    weighted = (mixing[None, :, :] * local_weights[:, None, :]).astype(BF16)

    me_at, core_at = at[:1], core.astype(jnp.int32)[None]

    def send(value, shift):
        return lax.ppermute(value, "context", [(i, (i + shift) % parts) for i in range(parts)])

    middle = parts // 2
    order = ((middle, 1, 1), (1, middle, 2))
    arrived = []
    for shifts in order:
        sent = reduced_parts(slices, context_factor, me_at, parts, shifts, BF16)
        arrived += [send(value, shifts[0] + shifts[1] * i) for i, value in enumerate(sent)]
    (own,) = reduced_parts(slices, context_factor, me_at, parts, (0, 1, 1), F32)
    inverse, mixing_gram, weight_gram = context_inverse(own, mixing, year_weights)
    own_rows, *shares = rows_and_gram(me_at, inverse, [own] + arrived, word_count)
    gram_part = sum_all([shares[0]] + [send(shares[shift], shift) for shift in range(1, parts)])
    rows = around(own_rows, "context")
    distance = 1
    while distance < word_count:
        partner = distance if 2 * distance < word_count else word_count - 1
        got = lax.ppermute(gram_part, "word", [(i, i ^ partner) for i in range(word_count)])
        distance *= 2
        gram_part = sum_all([gram_part, got], *(rows[1:] if distance == word_count else []))
    grams = around(gram_part, "context")

    keep, give, side_keep, side_give = frames_and_context(
        at, slices, grams, rows, coupled, weighted, year_weights, mixing
    )

    swap = [(i, cores - 1 - i) for i in range(cores)]
    count = x_count * word_count
    both = add_cores(keep, lax.ppermute(give, "core", swap)).reshape(count, -1, rank)
    factor_half = sum_all(around(factor_share(core_at, both, context_factor, cores), "context"))
    factor_other = lax.ppermute(factor_half, "core", swap)
    side_got = lax.ppermute(side_give, "core", swap)
    both_parts = lax.all_to_all(both, ("x", "word"), 0, 0, tiled=True)
    packed = pack_sum(both_parts, inverse, factor_other, side_got)
    first, second = factor_inverses(core_at, packed, mixing_gram, weight_gram, factor_half, factor_other)
    spread = jnp.broadcast_to(packed.astype(jnp.float16)[None], (count,) + packed.shape)
    mine = lax.all_to_all(spread, ("x", "word"), 0, 0, tiled=True)
    side_half = sum_all(around(sum_all([side_keep, side_got], packed), "x"), first)
    side_other = lax.ppermute(side_half, "core", swap)
    mine, side_other = lax.optimization_barrier((mine, side_other))
    new_mixing, new_years = solve_sides(core_at, packed, first, second, side_half, side_other)
    other = lax.ppermute(mine, "core", swap)
    new_context = unpack_into(core_at, mine.astype(F32), None)
    new_context = unpack_into(1 - core_at, other.astype(F32), new_context)
    return (new_mixing, new_context, new_years)


def solution(mesh):
    year_count, word_count, context_count = mesh.devices.shape
    cores = 2
    fine = Mesh(
        mesh.devices.reshape(year_count // cores, cores, word_count, context_count),
        ("x", "core", "word", "context"),
    )
    in_specs = (P(("x", "core"), "word", "context"), P("context", None), P(), P())
    out_specs = (P(), P("context", None), P())
    return jax.shard_map(local, mesh=fine, in_specs=in_specs, out_specs=out_specs, check_vma=False)
```
